256 devices in a mesh: dp: 4 (over y), head: 64 (over x, z, core).
Axes of the slice: x: 4, y: 4, z: 8, core: 2. Of those that a mesh axis runs over, the one named last changes fastest.
Arguments:
- unfinished: int32 [128], P('dp'), may hold values from 0 to 255, as said below
- states: bfloat16 [256, 64, 128, 128], P(('dp', 'head')), may hold values from -6 to 6
- qkv_rows: bfloat16 [256, 64, 4, 3, 128], P(('dp', 'head')), may hold values from -6 to 6
- decay_rate: float32 [64], P('head'), may hold values from 0.02 to 2
- out_weight: bfloat16 [8192, 6144], P('head'), may hold values from -0.1875 to 0.1875
- hidden_in: bfloat16 [6144, 128, 4], P('head', 'dp'), may hold values from -6 to 6
- routes: int32 [128, 4, 2], P('dp'), may hold values from 0 to 31, as said below
- route_weight: float32 [128, 4, 2], P('dp'), may hold values from 0.2 to 1
- expert_up: bfloat16 [4, 6144, 2, 9216], P('dp', None, None, 'head'), may hold values from -0.078125 to 0.078125
- expert_down: bfloat16 [4, 9216, 6144], P('dp', 'head'), may hold values from -0.1875 to 0.1875
Outputs:
- mixed: bfloat16 [6144, 128, 4], P('head', 'dp')
The draws below stay inside these ranges and needn't reach their ends.
Inputs may be any that keep to these rules, and one draw needn't show every extreme that they name: `unfinished`: entries are distinct, in no particular order. Data group g owns slots g * 64 to (g + 1) * 64 - 1; at most 48 entries fall in one group's slots, and exactly 48 in some group. `routes`: A token's two experts differ and at most one of them is below 4. Among the 128 tokens of one data group (aligned blocks of rows), each expert below 4 is named at most 16 times, and one of them exactly 16 times.
All inputs are finite; a program needn't handle non-finite values.
Results may differ from the reference program's by a relative error of at most 0.0044.
Values may be sent and summed in bfloat16 or wider, within the bound.
No kernel may reach another device: no remote copies, remote signals or barrier semaphores. Data moves between devices by JAX's collectives and lax.ppermute only.
A program may use at most 64 MiB of HBM per device.

```python
import math
import jax
import jax.numpy as jnp
from jax import lax

D = 6144
HEADS = 64
HD = 128
FF = 9216
EXPERTS = 32
STEPS = 4
SLOT_DEV = 1
SLOTS = 256
ROW_GRP = 32
ROWS = 128
CAP_GRP = 48
EXP_CAP = 16
FLIGHT = 4
N_DP = 4
N_HEAD = 64


def draw_unfinished(key, part):
    key = jax.random.fold_in(key, 11)
    key_shift, key_place, key_pick, key_mix = jax.random.split(key, 4)
    slot_grp = SLOT_DEV * N_HEAD
    others = N_DP - 1
    remain = ROWS - CAP_GRP
    base_count = remain // others
    extra = remain - base_count * others
    room_size = max(0, min(base_count - 1, CAP_GRP - base_count - extra) // 2)
    counts_rest = jnp.full((others,), base_count, jnp.int32).at[0].add(extra)
    shifts = jax.random.randint(key_shift, (others,), -room_size, room_size + 1)
    position = jnp.arange(others)
    pair_limit = others // 2 * 2
    signed = jnp.where(position < pair_limit, jnp.where(position % 2 == 0, 1, -1), 0)
    partner = jnp.where(position % 2 == 0, position, position - 1)
    counts_rest = counts_rest + signed * shifts[partner]
    heavy = jax.random.randint(key_place, (), 0, N_DP)
    groups = jnp.arange(N_DP)
    source = jnp.clip(groups - (groups > heavy).astype(jnp.int32), 0, others - 1)
    counts = jnp.where(groups == heavy, CAP_GRP, counts_rest[source])

    def one_order(group_key):
        return jax.random.permutation(group_key, slot_grp)
    orders = jax.vmap(one_order)(jax.random.split(key_pick, N_DP))
    slot_pos = jnp.arange(slot_grp)[None, :]
    orders = jnp.where(orders == 0, orders[:, -1:], jnp.where(slot_pos == slot_grp - 1, 0, orders))
    orders = jnp.where(orders == 1, orders[:, :1], jnp.where(slot_pos == 0, 1, orders))
    chosen = (orders < counts[:, None]).reshape(-1)
    sort_keys = jnp.where(chosen, 0, 1) * (N_DP * slot_grp) + jnp.arange(N_DP * slot_grp)
    picked = jnp.argsort(sort_keys)[:ROWS].astype(jnp.int32)
    mixing = jax.random.permutation(key_mix, ROWS)
    return picked[mixing].astype(jnp.int32)


def draw_routes(key, part):
    key = jax.random.fold_in(key, 23)
    tok_grp = ROW_GRP * STEPS
    others = EXPERTS - FLIGHT

    def one_group(group_key):
        keys = jax.random.split(group_key, 7)
        heavy = jax.random.randint(keys[0], (), 0, FLIGHT)
        loads = jax.random.randint(keys[1], (FLIGHT,), max(1, EXP_CAP // 4), EXP_CAP + 1)
        loads = jnp.where(jnp.arange(FLIGHT) == heavy, EXP_CAP, loads)
        lower = jnp.cumsum(loads) - loads
        order = jax.random.permutation(keys[2], tok_grp)
        inside = (order[:, None] >= lower[None, :]) & (order[:, None] < (lower + loads)[None, :])
        has_flight = jnp.any(inside, 1)
        flight_id = jnp.sum(inside.astype(jnp.int32) * jnp.arange(FLIGHT)[None, :], 1)
        first_off = jax.random.randint(keys[3], (tok_grp,), 0, others)
        first = jnp.where(has_flight, flight_id, FLIGHT + first_off)
        step_off = jax.random.randint(keys[4], (tok_grp,), 1, others)
        fresh = jax.random.randint(keys[5], (tok_grp,), 0, others)
        second = FLIGHT + jnp.where(has_flight, fresh, (first_off + step_off) % others)
        flip = jax.random.randint(keys[6], (tok_grp,), 0, 2)
        left = jnp.where(flip == 1, second, first)
        right = jnp.where(flip == 1, first, second)
        return jnp.stack([left, right], 1)
    grouped = jax.vmap(one_group)(jax.random.split(key, N_DP))
    return grouped.reshape(ROWS, STEPS, 2).astype(jnp.int32)


def raised(result, own_key, source, target, blocks, factor):
    def block_of(dim):
        return (jnp.arange(result.shape[dim]) // (result.shape[dim] // blocks)).reshape((-1,) + (1,) * (result.ndim - 1 - dim))

    one_side = jax.random.permutation(own_key, blocks)[block_of(target)]
    far = (block_of(target) + blocks // 2) % blocks
    return jnp.where((block_of(source) == one_side) | (block_of(source) == far), factor * result, result)


def steps_of(stream_key, shape, shards, least, largest):
    factor_of, own = 1.0, jax.random.fold_in(stream_key, 6)
    for dim, shards_of in shards:
        draws = jnp.exp(jax.random.uniform(jax.random.fold_in(own, dim), (shards_of,), jnp.float32, least / len(shards), largest / len(shards)))
        factor_of = factor_of * jnp.repeat(draws, shape[dim] // shards_of).reshape([-1 if axis == dim else 1 for axis in range(len(shape))])
    return factor_of


def noise(own_key, extent, width, bound, cuts=(), held_as=jnp.bfloat16):
    drawn = width * jax.random.normal(own_key, extent, jnp.float32)
    if cuts:
        drawn = drawn * steps_of(own_key, extent, cuts, -0.22, 0.18)
    return jnp.clip(drawn, -bound, bound).astype(held_as)


def noise_with(own_key, extent, spread, most, cuts, heavy, held_as=jnp.bfloat16):
    drawn = spread * jax.random.normal(own_key, extent, jnp.float32)
    if cuts:
        drawn = drawn * steps_of(own_key, extent, cuts, -0.22, 0.18)
    return jnp.clip(raised(drawn, jax.random.fold_in(own_key, 3), *heavy), -most, most).astype(held_as)


def setup_inputs(seed: int = 0) -> dict:
    seeds = jax.random.split(jax.random.key(seed), 11)
    unfinished = draw_unfinished(jax.random.fold_in(seeds[10], 71), 0)
    states = noise(seeds[1], (SLOTS, HEADS, HD, HD), 1.0, 6.0, ((0, 256),))
    qkv_rows = noise(seeds[2], (SLOTS, HEADS, STEPS, 3, HD), 1.0, 6.0, ((0, 256),))
    decay_rate = jnp.clip(jnp.exp(math.log(2.0) - 4.6051702 * jax.random.uniform(seeds[3], (HEADS,), jnp.float32) ** steps_of(seeds[3], (HEADS,), ((0, 64),), -0.2, 0.2)), 0.02, 2.0)
    out_weight = noise_with(seeds[4], (HEADS * HD, D), (HEADS * HD) ** -0.5, 0.1875, ((0, 64),), (0, 1, 64, 4.0))
    hidden_in = noise(seeds[5], (D, ROWS, STEPS), 1.0, 6.0, ((0, 64), (1, 4)))
    routes = draw_routes(jax.random.fold_in(seeds[10], 71), 0)
    route_weight = jnp.clip(0.2 + 0.8 * jax.random.uniform(seeds[7], (ROWS, STEPS, 2), jnp.float32) ** steps_of(seeds[7], (ROWS, STEPS, 2), ((0, 4),), -0.2, 0.2), 0.2, 1.0)
    expert_up = noise(seeds[8], (FLIGHT, D, 2, FF), D ** -0.5, 0.078125, ((0, 4), (3, 64)))
    expert_down = noise_with(seeds[9], (FLIGHT, FF, D), FF ** -0.5, 0.1875, ((0, 4), (1, 64)), (1, 2, 64, 4.0))
    return dict(unfinished=unfinished, states=states, qkv_rows=qkv_rows, decay_rate=decay_rate, out_weight=out_weight, hidden_in=hidden_in, routes=routes, route_weight=route_weight, expert_up=expert_up, expert_down=expert_down)


EPSILON_HEAD = 1e-06
EPSILON_NORM = 1e-05

def lightning(state_rows, input_rows, rate_vec):
    factor = jnp.exp(-rate_vec)[None, :, None, None]
    memory = state_rows.astype(jnp.float32)
    outputs = []
    for step_index in range(input_rows.shape[2]):
        query_vec = jax.nn.silu(input_rows[:, :, step_index, 0].astype(jnp.float32))
        key_vec = jax.nn.silu(input_rows[:, :, step_index, 1].astype(jnp.float32))
        value_vec = input_rows[:, :, step_index, 2].astype(jnp.float32)
        memory = factor * memory + key_vec[..., :, None] * value_vec[..., None, :]
        outputs.append(jnp.einsum('rhe,rhef->rhf', query_vec, memory, precision=lax.Precision.HIGHEST))
    stacked = jnp.stack(outputs, 2)
    scaled = stacked * lax.rsqrt(lax.optimization_barrier(jnp.mean(stacked * stacked, -1, keepdims=True)) + EPSILON_HEAD)
    return scaled.astype(jnp.bfloat16)

def reference(unfinished, states, qkv_rows, decay_rate, out_weight, hidden_in, routes, route_weight, expert_up, expert_down):
    row_total = unfinished.shape[0]

    def one_row(slot_index):
        state_one = lax.dynamic_index_in_dim(states, slot_index, 0, keepdims=True)
        input_one = lax.dynamic_index_in_dim(qkv_rows, slot_index, 0, keepdims=True)
        return lightning(state_one, input_one, decay_rate)[0]
    attended = lax.map(one_row, unfinished)
    head_flat = attended.transpose(0, 2, 1, 3).reshape(row_total * STEPS, HEADS * HD)
    projected = jnp.dot(head_flat, out_weight, preferred_element_type=jnp.float32)
    residual = hidden_in.reshape(D, row_total * STEPS).T.astype(jnp.float32) + projected
    normed = (residual * lax.rsqrt(lax.optimization_barrier(jnp.mean(residual * residual, 1, keepdims=True)) + EPSILON_NORM)).astype(jnp.bfloat16)
    tok_grp = ROW_GRP * STEPS
    buffer_len = N_DP * EXP_CAP
    flat_routes = routes.reshape(N_DP, tok_grp * 2)
    one_hot = (flat_routes[..., None] == jnp.arange(FLIGHT)[None, None, :]).astype(jnp.int32)
    ranking = lax.optimization_barrier(jnp.sum((jnp.cumsum(one_hot, 1) - one_hot) * one_hot, 2))
    in_flight = flat_routes < FLIGHT
    group_ids = jnp.arange(N_DP)[:, None]
    token_ids = group_ids * tok_grp + jnp.arange(tok_grp * 2)[None, :] // 2
    buffer_pos = jnp.where(in_flight, flat_routes * buffer_len + group_ids * EXP_CAP + ranking, FLIGHT * buffer_len)
    token_of = jnp.zeros((FLIGHT * buffer_len,), jnp.int32).at[buffer_pos.reshape(-1)].set(token_ids.reshape(-1).astype(jnp.int32), mode='drop')

    def one_expert(expert_id):
        chosen = lax.dynamic_slice_in_dim(token_of, expert_id * buffer_len, buffer_len, 0)
        inputs = jnp.take(normed, chosen, 0)
        weight_in = lax.dynamic_index_in_dim(expert_up, expert_id, 0, keepdims=False).reshape(D, 2 * FF)
        gate_up = jnp.dot(inputs, weight_in, preferred_element_type=jnp.float32)
        expert_hidden = (jax.nn.silu(gate_up[:, :FF]) * gate_up[:, FF:]).astype(jnp.bfloat16)
        weight_out = lax.dynamic_index_in_dim(expert_down, expert_id, 0, keepdims=False)
        return jnp.dot(expert_hidden, weight_out, preferred_element_type=jnp.float32).astype(jnp.bfloat16)
    expert_result = lax.map(one_expert, jnp.arange(FLIGHT)).reshape(FLIGHT * buffer_len, D)
    safe_pos = jnp.minimum(buffer_pos, FLIGHT * buffer_len - 1).reshape(-1)
    fetched = jnp.take(expert_result, safe_pos, 0).astype(jnp.float32).reshape(N_DP, tok_grp, 2, D)
    weights = jnp.where(in_flight, route_weight.reshape(N_DP, tok_grp * 2), 0.0).reshape(N_DP, tok_grp, 2, 1)
    expert_mix = lax.optimization_barrier(jnp.sum(fetched * weights, 2)).reshape(row_total * STEPS, D)
    return (residual + expert_mix).T.reshape(D, row_total, STEPS).astype(jnp.bfloat16)
```

```python
import functools

import jax
import jax.numpy as jnp
from jax import lax
from jax.experimental import pallas as pl
from jax.experimental.pallas import tpu as pltpu
from jax.sharding import Mesh, PartitionSpec as P

EPSILON_HEAD = 1e-06
EPSILON_NORM = 1e-05
BF16, F32 = jnp.bfloat16, jnp.float32
NX, NZ, NC = 4, 8, 2
EVERY = ("dp", "x", "z", "core")
HEAD = ("x", "z", "core")
MIB = 1 << 20


def vmem_spec():
    return pl.BlockSpec(memory_space=pltpu.VMEM)


def params(mib=48):
    return pltpu.CompilerParams(vmem_limit_bytes=mib * MIB)


def nt_dot(left, right):
    return lax.dot_general(left, right, (((1,), (1,)), ((), ())), preferred_element_type=F32)


def silu(value):
    return value / (1.0 + jnp.exp(-value))


def attend_kernel(state_ref, input_ref, base_ref, cross_ref):
    heads = state_ref.shape[0]
    query = silu(input_ref[:, 0].astype(F32))
    key = silu(input_ref[:, 1].astype(F32))
    value = input_ref[:, 2].astype(F32)
    high = query.astype(BF16)
    low = (query - high.astype(F32)).astype(BF16)
    for head in range(heads):
        state = state_ref[head]
        base_ref[head] = jnp.dot(high[head], state, preferred_element_type=F32) + jnp.dot(
            low[head], state, preferred_element_type=F32
        )
    for source in range(4):
        weight = jnp.sum(query * key[:, source : source + 1], -1, keepdims=True)
        cross_ref[source] = weight * value[:, source : source + 1]


def attend(states, inputs):
    heads, block = states.shape[0], 8
    return pl.pallas_call(
        attend_kernel,
        grid=(heads // block,),
        in_specs=[
            pl.BlockSpec((block, 128, 128), lambda i: (i, 0, 0)),
            pl.BlockSpec((block, 3, 4, 128), lambda i: (i, 0, 0, 0)),
        ],
        out_specs=[
            pl.BlockSpec((block, 4, 128), lambda i: (i, 0, 0)),
            pl.BlockSpec((4, block, 4, 128), lambda i: (0, i, 0, 0)),
        ],
        out_shape=[
            jax.ShapeDtypeStruct((heads, 4, 128), F32),
            jax.ShapeDtypeStruct((4, heads, 4, 128), F32),
        ],
        cost_estimate=pl.CostEstimate(flops=2 * 8 * 64 * 128 * 128, bytes_accessed=3 * MIB, transcendentals=65536),
        compiler_params=params(),
        name="attend",
    )(states, inputs)


def decay_kernel(base_ref, cross_ref, rate_ref, out_ref):
    rate = rate_ref[...]
    shape = base_ref.shape
    step = lax.broadcasted_iota(jnp.int32, shape, 1)
    stepf = step.astype(F32)
    attn = jnp.exp(-rate * (stepf + 1.0)) * base_ref[...]
    for source in range(4):
        lag = jnp.maximum(stepf - source, 0.0)
        attn += jnp.where(step >= source, jnp.exp(-rate * lag), 0.0) * cross_ref[source]
    scaled = attn * lax.rsqrt(jnp.mean(attn * attn, -1, keepdims=True) + EPSILON_HEAD)
    scaled = scaled.astype(BF16)
    for copy in range(out_ref.shape[0]):
        out_ref[copy] = scaled


def decay_heads(base, cross, rates, copies):
    return pl.pallas_call(
        decay_kernel,
        in_specs=[vmem_spec()] * 3,
        out_specs=vmem_spec(),
        out_shape=jax.ShapeDtypeStruct((copies,) + base.shape, BF16),
        compiler_params=params(),
        name="decay_heads",
    )(base, cross, rates)


def split_out_kernel(core_ref, weight_ref, keep_ref, send_ref):
    core = core_ref[0]
    weight = weight_ref[...]
    row = lax.broadcasted_iota(jnp.int32, (192, 384), 0)
    lane = lax.broadcasted_iota(jnp.int32, (192, 384), 1)
    for parity, out_ref in ((core, keep_ref), (1 - core, send_ref)):
        source = (row // 96) * 192 + row % 96 + parity * 96
        pick = (lane == source).astype(F32).astype(BF16)
        out_ref[...] = nt_dot(pick, weight).astype(BF16).reshape(out_ref.shape)


def split_out(core, weight):
    shape = jax.ShapeDtypeStruct((32, 96, 128), BF16)
    return pl.pallas_call(
        split_out_kernel,
        grid=(16,),
        in_specs=[
            pl.BlockSpec(memory_space=pltpu.SMEM),
            pl.BlockSpec((128, 384), lambda i: (0, i)),
        ],
        out_specs=[pl.BlockSpec((2, 96, 128), lambda i: (i, 0, 0))] * 2,
        out_shape=[shape, shape],
        cost_estimate=pl.CostEstimate(flops=2 * 16 * 384 * 384 * 128, bytes_accessed=3 * MIB, transcendentals=0),
        compiler_params=params(),
        name="split_out",
    )(core, weight)


def split_down_kernel(core_ref, weight_ref, keep_ref, send_ref):
    core = core_ref[0]
    weight = weight_ref[...]
    row = lax.broadcasted_iota(jnp.int32, (384, 256), 0)
    lane = lax.broadcasted_iota(jnp.int32, (384, 256), 1)
    for parity, out_ref in ((core, keep_ref), (1 - core, send_ref)):
        source = (lane // 128) * 192 + lane % 128 + parity * 96
        pick = ((row == source) & (lane % 128 < 96)).astype(F32).astype(BF16)
        out_ref[...] = jnp.dot(weight, pick, preferred_element_type=F32).astype(BF16)


def split_down(core, weight):
    hidden = weight.shape[0]
    shape = jax.ShapeDtypeStruct((hidden, 4096), BF16)
    return pl.pallas_call(
        split_down_kernel,
        grid=(16,),
        in_specs=[
            pl.BlockSpec(memory_space=pltpu.SMEM),
            pl.BlockSpec((hidden, 384), lambda i: (0, i)),
        ],
        out_specs=[pl.BlockSpec((hidden, 256), lambda i: (0, i))] * 2,
        out_shape=[shape, shape],
        cost_estimate=pl.CostEstimate(flops=2 * 16 * 384 * 512 * 144, bytes_accessed=4 * MIB, transcendentals=0),
        compiler_params=params(),
        name="split_down",
    )(core, weight)


def project_kernel(keep_ref, other_ref, mine_ref, theirs_ref, out_ref):
    blocks = keep_ref.shape[0]
    mine = mine_ref[...]
    theirs = theirs_ref[...]
    mine = jnp.concatenate([mine, mine[128:]], 0)
    theirs = jnp.concatenate([theirs, theirs[128:]], 0)
    total = nt_dot(keep_ref[...].reshape(blocks * 96, 128), mine) + nt_dot(
        other_ref[...].reshape(blocks * 96, 128), theirs
    )
    total = total.reshape(blocks, 96, 256)
    left = lax.broadcasted_iota(jnp.int32, (blocks, 48, 128), 2) < 64
    out_ref[:, :96] = total[:, :, :128].astype(BF16)
    out_ref[:, 96:] = jnp.where(left, total[:, :48, 128:], total[:, 48:, 128:]).astype(BF16)


def project(keep, other, mine, theirs):
    block = 8
    weights = pl.BlockSpec((block, 96, 128), lambda i: (i, 0, 0))
    tokens = pl.BlockSpec((192, 128), lambda i: (0, 0))
    return pl.pallas_call(
        project_kernel,
        grid=(32 // block,),
        in_specs=[weights, weights, tokens, tokens],
        out_specs=pl.BlockSpec((block, 144, 128), lambda i: (i, 0, 0)),
        out_shape=jax.ShapeDtypeStruct((32, 144, 128), BF16),
        compiler_params=params(),
        name="project",
    )(keep, other, mine, theirs)


def add_kernel(in_ref, out_ref):
    out_ref[...] = jnp.sum(in_ref[...].astype(F32), 0).astype(BF16)


def add_parts(parts):
    block = parts.shape[1] // 4
    return pl.pallas_call(
        add_kernel,
        grid=(4,),
        in_specs=[pl.BlockSpec((parts.shape[0], block, 128), lambda i: (0, i, 0))],
        out_specs=pl.BlockSpec((block, 128), lambda i: (i, 0)),
        out_shape=jax.ShapeDtypeStruct(parts.shape[1:], BF16),
        compiler_params=params(),
        name="add_parts",
    )(parts)


def residual_kernel(in_ref, hidden_ref, own_ref, send_ref):
    total = jnp.sum(in_ref[...].astype(F32), 0)
    own_ref[...] = total[:96]
    routed = (total[96:] + hidden_ref[...]).astype(BF16)
    for copy in range(send_ref.shape[0]):
        send_ref[copy] = routed


def residual_parts(parts, hidden, copies):
    return pl.pallas_call(
        residual_kernel,
        in_specs=[vmem_spec()] * 2,
        out_specs=[vmem_spec()] * 2,
        out_shape=[
            jax.ShapeDtypeStruct((96, 128), F32),
            jax.ShapeDtypeStruct((copies, 48, 128), BF16),
        ],
        compiler_params=params(),
        name="residual_parts",
    )(parts, hidden)


def up_kernel(core_ref, mine_ref, theirs_ref, weight_ref, out_ref, total_ref, square_ref):
    index = pl.program_id(0)
    even = core_ref[0] == 0
    blocks = mine_ref.shape[0]
    mine, theirs = mine_ref[...], theirs_ref[...]
    first = jnp.where(even, mine, theirs)
    second = jnp.where(even, theirs, mine)
    left = lax.broadcasted_iota(jnp.int32, (48, 128), 1) < 64
    zero = jnp.zeros((48, 128), BF16)
    pieces = []
    for block in range(blocks):
        for part in (first, second):
            pieces += [jnp.where(left, part[block], zero), jnp.where(left, zero, part[block])]
    tokens = jnp.concatenate(pieces, 0)

    @pl.when(index == 0)
    def _():
        total_ref[...] = jnp.zeros_like(total_ref)
        square_ref[...] = jnp.zeros_like(square_ref)

    total_ref[...] += jnp.dot(weight_ref[...], tokens, preferred_element_type=F32)
    wide = tokens.astype(F32)
    square_ref[...] += jnp.sum((wide * wide).reshape(-1, 8, 128), 0)

    @pl.when(index == pl.num_programs(0) - 1)
    def _():
        total, square = total_ref[...], jnp.sum(square_ref[...], 0, keepdims=True)
        total = total[:, :64] + total[:, 64:]
        square = square[:, :64] + square[:, 64:]
        total = total * lax.rsqrt(square / 6144.0 + EPSILON_NORM)
        half = total.shape[0] // 2
        out_ref[...] = (silu(total[:half]) * total[half:]).astype(BF16)


def up_project(core, mine, theirs, weight):
    rows, width = weight.shape
    steps = 4
    tokens = pl.BlockSpec((32 // steps, 48, 128), lambda i: (i, 0, 0))
    return pl.pallas_call(
        up_kernel,
        grid=(steps,),
        in_specs=[
            pl.BlockSpec(memory_space=pltpu.SMEM),
            tokens,
            tokens,
            pl.BlockSpec((rows, width // steps), lambda i: (0, i)),
        ],
        out_specs=pl.BlockSpec((rows // 2, 64), lambda i: (0, 0)),
        out_shape=jax.ShapeDtypeStruct((rows // 2, 64), BF16),
        scratch_shapes=[pltpu.VMEM((rows, 128), F32), pltpu.VMEM((8, 128), F32)],
        compiler_params=params(),
        name="up_project",
    )(core, mine, theirs, weight)


def down_kernel(mine_ref, theirs_ref, keep_ref, other_ref, out_ref):
    dims = (((0,), (0,)), ((), ()))
    total = lax.dot_general(
        mine_ref[...], keep_ref[...], dims, preferred_element_type=F32
    ) + lax.dot_general(theirs_ref[...], other_ref[...], dims, preferred_element_type=F32)
    total = total.astype(BF16)
    for block in range(out_ref.shape[1]):
        out_ref[:, block] = total[:, block * 128 : block * 128 + 128].reshape(4, 16, 128)


def down_project(mine, theirs, keep, other):
    hidden = mine.shape[0]
    steps = 4
    tokens = pl.BlockSpec((hidden, 64), lambda i: (0, 0))
    weights = pl.BlockSpec((hidden, 4096 // steps), lambda i: (0, i))
    return pl.pallas_call(
        down_kernel,
        grid=(steps,),
        in_specs=[tokens, tokens, weights, weights],
        out_specs=pl.BlockSpec((4, 32 // steps, 16, 128), lambda i: (0, i, 0, 0)),
        out_shape=jax.ShapeDtypeStruct((4, 32, 16, 128), BF16),
        compiler_params=params(),
        name="down_project",
    )(mine, theirs, keep, other)


def combine_kernel(parts_ref, place_ref, weight_ref, residual_ref, out_ref):
    result = jnp.sum(parts_ref[...].astype(F32), 1).astype(BF16).reshape(64, 128)
    fetched = jnp.dot(place_ref[...], result, preferred_element_type=F32)
    out_ref[...] = (residual_ref[...] + weight_ref[...] * fetched[:, :96]).astype(BF16)


def combine(parts, place, weight, residual):
    return pl.pallas_call(
        combine_kernel,
        in_specs=[vmem_spec()] * 4,
        out_specs=vmem_spec(),
        out_shape=jax.ShapeDtypeStruct((128, 96), BF16),
        compiler_params=params(),
        name="combine",
    )(parts, place, weight, residual)


def per_device(
    unfinished, states, qkv_rows, decay_rate, out_weight, hidden_in, routes, route_weight, expert_up, expert_down
):
    core = lax.axis_index("core").astype(jnp.int32).reshape(1)
    swap = functools.partial(lax.ppermute, axis_name="core", perm=[(0, 1), (1, 0)])

    with jax.named_scope("rates"):
        rates = lax.all_to_all(jnp.broadcast_to(decay_rate[:, None, None], (64, 1, 128)), HEAD, 0, 0, tiled=True)
    with jax.named_scope("attention"):
        base, cross = attend(states[0], qkv_rows[0].transpose(0, 2, 1, 3))

    with jax.named_scope("routing"):
        hidden = hidden_in.transpose(1, 2, 0).reshape(128, 96)
        pair = routes.reshape(128, 2)
        flying = pair < 4
        expert = jnp.min(pair, 1)
        weight = jnp.sum(jnp.where(flying, route_weight.reshape(128, 2), 0.0), 1, keepdims=True)
        named = (expert[:, None] == jnp.arange(4)[None, :]).astype(F32)
        before = jnp.arange(128)[:, None] > jnp.arange(128)[None, :]
        ranks = jnp.dot(before.astype(BF16), named.astype(BF16), preferred_element_type=F32)
        rank = jnp.sum(ranks * named, 1).astype(jnp.int32)
        position = jnp.where(expert < 4, expert * 16 + rank, -1)
        place = (position[:, None] == jnp.arange(64)[None, :]).astype(BF16)
        slots = jnp.repeat(unfinished, 4)
        steps = jnp.tile(jnp.arange(4), 32)
        facts = jnp.concatenate(
            [
                hidden,
                slots[:, None].astype(BF16),
                steps[:, None].astype(BF16),
                jnp.zeros((128, 30), BF16),
            ],
            1,
        )
        packed = lax.dot_general(place, facts, (((0,), (0,)), ((), ())), preferred_element_type=F32).astype(BF16)
        routed = lax.all_to_all(packed.reshape(4, 16, 128), "dp", 0, 0, tiled=True).reshape(64, 128)
        routed_index = (routed[:, 96].astype(F32) * 4.0 + routed[:, 97].astype(F32)).astype(jnp.int32)
        index = jnp.concatenate([slots * 4 + steps, routed_index])
        pick = (index[:, None] == jnp.arange(1024)[None, :]).astype(BF16)
        routed_hidden = routed[:, :96].astype(F32).T
        routed_hidden = jnp.concatenate([routed_hidden[:48], routed_hidden[48:]], 1)

    with jax.named_scope("weights"):
        keep_out, send_out = split_out(core, out_weight)
        other_out = swap(send_out)
        keep_down, send_down = split_down(core, expert_down[0])
        other_down = swap(send_down)

    with jax.named_scope("heads"):
        head_out = decay_heads(base, cross, rates, 4).reshape(256, 4, 128)
        head_rows = lax.all_to_all(head_out, EVERY, 0, 0, tiled=True).reshape(1024, 128)
        mine = jnp.dot(pick, head_rows, preferred_element_type=F32).astype(BF16)
        theirs = swap(mine)
    with jax.named_scope("projection"):
        partial = project(keep_out, other_out, mine, theirs)
        over_x = lax.all_to_all(partial.reshape(NX, NZ * 144, 128), "x", 0, 0, tiled=True)
        over_z = lax.all_to_all(add_parts(over_x).reshape(NZ, 144, 128), "z", 0, 0, tiled=True)
        own, routed_send = residual_parts(over_z, routed_hidden, NX * NZ)
    with jax.named_scope("expert"):
        features = lax.all_to_all(routed_send, ("x", "z"), 0, 0, tiled=True)
        up = expert_up[0].transpose(1, 2, 0).reshape(288, 6144)
        expert_hidden = up_project(core, features, swap(features), up)
        results = down_project(expert_hidden, swap(expert_hidden), keep_down, other_down)
        returned = lax.all_to_all(results.reshape(128, 16, 128), ("dp", "x", "z"), 0, 0, tiled=True)
    with jax.named_scope("output"):
        residual = own.T + hidden.astype(F32)
        mixed = combine(returned.reshape(4, 32, 16, 128), place, weight, residual)
        return mixed.reshape(32, 4, 96).transpose(2, 0, 1)


def solution(mesh):
    grid = Mesh(mesh.devices.reshape(mesh.shape["dp"], NX, NZ, NC), EVERY)
    return jax.shard_map(
        per_device,
        mesh=grid,
        in_specs=(
            P("dp"),
            P(EVERY, None, None, None),
            P(EVERY, None, None, None, None),
            P(HEAD),
            P(HEAD, None),
            P(HEAD, "dp", None),
            P("dp", None, None),
            P("dp", None, None),
            P("dp", None, None, HEAD),
            P("dp", HEAD, None),
        ),
        out_specs=P(HEAD, "dp", None),
        check_vma=False,
    )
```

```python
import functools

import jax
import jax.numpy as jnp
from jax import lax
from jax.experimental import pallas as pl
from jax.experimental.pallas import tpu as pltpu
from jax.sharding import Mesh, PartitionSpec as P

EPSILON_HEAD = 1e-06
EPSILON_NORM = 1e-05
BF16, F32 = jnp.bfloat16, jnp.float32
NX, NZ, NC = 4, 8, 2
EVERY = ("dp", "x", "z", "core")
HEAD = ("x", "z", "core")
MIB = 1 << 20


def vmem_spec():
    return pl.BlockSpec(memory_space=pltpu.VMEM)


def smem_spec():
    return pl.BlockSpec(memory_space=pltpu.SMEM)


def any_spec():
    return pl.BlockSpec(memory_space=pl.ANY)


def in_hbm(value):
    return pltpu.with_memory_space_constraint(value, pltpu.HBM)


def params(mib=12):
    return pltpu.CompilerParams(vmem_limit_bytes=mib * MIB)


def cost(flops, size):
    return pl.CostEstimate(flops=flops, bytes_accessed=size, transcendentals=0)


def shape(dims, dtype=BF16):
    return jax.ShapeDtypeStruct(dims, dtype)


def nt_dot(left, right):
    return lax.dot_general(left, right, (((1,), (1,)), ((), ())), preferred_element_type=F32)


def tn_dot(left, right):
    return lax.dot_general(left, right, (((0,), (0,)), ((), ())), preferred_element_type=F32)


def silu(value):
    return value / (1.0 + jnp.exp(-value))


def one_hot(mask):
    return mask.astype(F32).astype(BF16)


def attend_kernel(state_ref, input_ref, out_ref):
    heads = state_ref.shape[0]
    query = silu(input_ref[:, 0].astype(F32))
    key = silu(input_ref[:, 1].astype(F32))
    high = query.astype(BF16).astype(F32)
    both = jnp.concatenate([high, query - high], 1).astype(BF16)
    for head in range(heads):
        base = jnp.dot(both[head], state_ref[head], preferred_element_type=F32)
        out_ref[head, 0] = (base[:4] + base[4:]).astype(BF16)
    out_ref[:, 1] = input_ref[:, 2]
    lane = lax.broadcasted_iota(jnp.int32, query.shape, 2)
    cross = jnp.zeros(query.shape, F32)
    for source in range(4):
        weight = jnp.sum(query * key[:, source : source + 1], -1, keepdims=True)
        whole = weight.astype(BF16).astype(F32)
        cross = jnp.where(lane == source, whole, cross)
        cross = jnp.where(lane == source + 4, weight - whole, cross)
    out_ref[:, 2] = cross.astype(BF16)


def attend(states, inputs):
    heads, block = states.shape[0], 16
    return pl.pallas_call(
        attend_kernel,
        grid=(heads // block,),
        in_specs=[
            pl.BlockSpec((block, 128, 128), lambda i: (i, 0, 0)),
            pl.BlockSpec((block, 3, 4, 128), lambda i: (i, 0, 0, 0)),
        ],
        out_specs=pl.BlockSpec((block, 3, 4, 128), lambda i: (i, 0, 0, 0)),
        out_shape=shape((heads, 3, 4, 128)),
        cost_estimate=cost(2 * 8 * 64 * 128 * 128, 3 * MIB),
        compiler_params=params(),
        name="attend",
    )(in_hbm(states), inputs)


def decay_kernel(rate_ref, parts_ref, facts_ref, after_ref, out_ref):
    slots = parts_ref.shape[0]
    rate = jnp.full((4, 128), rate_ref[0], F32)
    step = lax.broadcasted_iota(jnp.int32, (4, 128), 0).astype(F32)
    value = parts_ref[:, 1].astype(F32)
    cross = parts_ref[:, 2].astype(F32)
    cross += pltpu.roll(cross, 124, 2)
    attn = jnp.exp(-rate * (step + 1.0)) * parts_ref[:, 0].astype(F32)
    for source in range(4):
        factor = jnp.where(step >= source, jnp.exp(-rate * jnp.maximum(step - source, 0.0)), 0.0)
        attn += (factor * cross[:, :, source : source + 1]) * value[:, source : source + 1]
    scaled = attn * lax.rsqrt(jnp.mean(attn * attn, -1, keepdims=True) + EPSILON_HEAD)
    scaled = scaled.astype(BF16)
    for group in range(out_ref.shape[0]):
        out_ref[group, :slots] = scaled
        out_ref[group, slots:] = facts_ref[group]


def decay_heads(rate, parts, facts, after):
    slots = parts.shape[0]
    return pl.pallas_call(
        decay_kernel,
        in_specs=[smem_spec(), vmem_spec(), vmem_spec(), any_spec()],
        out_specs=vmem_spec(),
        out_shape=shape((4, slots + 4, 4, 128)),
        cost_estimate=cost(4 * MIB, MIB),
        compiler_params=params(),
        name="decay_heads",
    )(rate, parts, facts, after)


def route_kernel(pair_ref, weight_ref, hidden_ref, row_ref, place_ref, factor_ref, out_ref):
    pair = pair_ref[...]
    expert = jnp.min(pair, 1, keepdims=True)
    factor_ref[...] = jnp.sum(jnp.where(pair < 4, weight_ref[...], 0.0), 1, keepdims=True)
    token = lax.broadcasted_iota(jnp.int32, (128, 128), 0)
    lane = lax.broadcasted_iota(jnp.int32, (128, 128), 1)
    named = (lane == expert).astype(F32)
    ranks = jnp.dot(one_hot(token > lane), named.astype(BF16), preferred_element_type=F32)
    rank = jnp.sum(ranks * named, 1, keepdims=True).astype(jnp.int32)
    position = jnp.where(expert < 4, expert * 16 + rank, -1)
    place = one_hot(lane == position)
    place_ref[...] = place
    row = row_ref[...].astype(F32)
    facts = hidden_ref[...].astype(F32)
    facts = jnp.where(lane == 96, row, jnp.where(lane == 97, (token % 4).astype(F32), facts))
    slots = jnp.where(lane == 98, row, 0.0)
    quarter = one_hot((token % 16 < 8) & (lane == (token // 16 * 8 + token % 16) * 4))
    packed = tn_dot(place, facts.astype(BF16)) + jnp.dot(quarter, slots.astype(BF16), preferred_element_type=F32)
    out_ref[...] = packed[:64].reshape(4, 4, 4, 128).astype(BF16)


def route(pair, weight, hidden, row):
    return pl.pallas_call(
        route_kernel,
        in_specs=[vmem_spec()] * 4,
        out_specs=[vmem_spec()] * 3,
        out_shape=[shape((128, 128)), shape((128, 1), F32), shape((4, 4, 4, 128))],
        cost_estimate=cost(8 * MIB, MIB // 2),
        compiler_params=params(),
        name="route",
    )(pair, weight, hidden, row)


def select_kernel(rows_ref, out_ref, hidden_ref):
    span = rows_ref.shape[0] // 4
    steps = span - 16
    facts = jnp.concatenate([rows_ref[group * span + steps : (group + 1) * span] for group in range(4)], 0)
    held = facts.astype(F32)
    token = lax.broadcasted_iota(jnp.int32, (128, 64), 0)
    source = lax.broadcasted_iota(jnp.int32, (128, 64), 1)
    spread = one_hot(source == token // 32 * 16 + token % 32 // 4)
    rest = jnp.dot(spread, facts, preferred_element_type=F32)
    step = (lax.broadcasted_iota(jnp.int32, (128, 1), 0) % 4).astype(F32)
    row = jnp.concatenate([held[:, 96:97], rest[:, 98:99]], 0)
    step = jnp.concatenate([held[:, 97:98], step], 0)
    row = (row * 4.0 + step).astype(jnp.int32)
    row = row // steps * span + row % steps
    lane = lax.broadcasted_iota(jnp.int32, (192, rows_ref.shape[0]), 1)
    out_ref[...] = jnp.dot(one_hot(lane == row), rows_ref[...], preferred_element_type=F32).astype(BF16)
    turned = jnp.concatenate([held, held], 0).T
    left = lax.broadcasted_iota(jnp.int32, (48, 128), 1) < 64
    hidden_ref[...] = jnp.where(left, turned[:48], turned[48:96])


def select(rows):
    return pl.pallas_call(
        select_kernel,
        in_specs=[vmem_spec()],
        out_specs=[vmem_spec()] * 2,
        out_shape=[shape((192, 128)), shape((48, 128), F32)],
        cost_estimate=cost(2 * 192 * 1088 * 128, MIB),
        compiler_params=params(),
        name="select",
    )(rows)


def split_out_kernel(where_ref, mine_ref, theirs_ref, after_ref, *out_refs):
    core = where_ref[0]
    row = lax.broadcasted_iota(jnp.int32, (192, 384), 0)
    lane = lax.broadcasted_iota(jnp.int32, (192, 384), 1)
    pick = one_hot(lane == row // 96 * 192 + row % 96 + core * 96)
    for part in range(4):
        for weight_ref, out_ref in zip((mine_ref, theirs_ref), out_refs):
            weight = weight_ref[:, part * 384 : part * 384 + 384]
            out_ref[2 * part : 2 * part + 2] = nt_dot(pick, weight).astype(BF16).reshape(2, 96, 128)


def split_out(where, mine, theirs, after):
    return pl.pallas_call(
        split_out_kernel,
        grid=(4,),
        in_specs=[smem_spec()] + [pl.BlockSpec((128, 1536), lambda i: (0, i))] * 2 + [any_spec()],
        out_specs=[pl.BlockSpec((8, 96, 128), lambda i: (i, 0, 0))] * 2,
        out_shape=[shape((NX * NZ, 96, 128))] * 2,
        cost_estimate=cost(2 * 16 * 384 * 384 * 128, 3 * MIB),
        compiler_params=params(),
        name="split_out",
    )(where, mine, in_hbm(theirs), after)


def split_down_kernel(where_ref, mine_ref, theirs_ref, after_ref, *out_refs):
    core = where_ref[0]
    row = lax.broadcasted_iota(jnp.int32, (384, 256), 0)
    lane = lax.broadcasted_iota(jnp.int32, (384, 256), 1)
    pick = one_hot((row == lane // 128 * 192 + lane % 128 + core * 96) & (lane % 128 < 96))
    for part in range(4):
        for weight_ref, out_ref in zip((mine_ref, theirs_ref), out_refs):
            weight = weight_ref[:, part * 384 : part * 384 + 384]
            total = jnp.dot(weight, pick, preferred_element_type=F32)
            out_ref[:, part * 256 : part * 256 + 256] = total.astype(BF16)


def split_down(where, mine, theirs, after):
    hidden = mine.shape[0]
    return pl.pallas_call(
        split_down_kernel,
        grid=(4,),
        in_specs=[smem_spec()] + [pl.BlockSpec((hidden, 1536), lambda i: (0, i))] * 2 + [any_spec()],
        out_specs=[pl.BlockSpec((hidden, 1024), lambda i: (0, i))] * 2,
        out_shape=[shape((hidden, NX * NZ * 128))] * 2,
        cost_estimate=cost(2 * 16 * 384 * 512 * 144, 4 * MIB),
        compiler_params=params(),
        name="split_down",
    )(where, mine, in_hbm(theirs), after)


def project_kernel(keep_ref, other_ref, mine_ref, theirs_ref, out_ref):
    blocks = keep_ref.shape[0]
    mine, theirs = mine_ref[:64], theirs_ref[:64]
    total = nt_dot(keep_ref[...].reshape(blocks * 96, 128), jnp.concatenate([mine, mine], 0))
    total += nt_dot(other_ref[...].reshape(blocks * 96, 128), jnp.concatenate([theirs, theirs], 0))
    total = total.reshape(blocks, 96, 128)
    left = lax.broadcasted_iota(jnp.int32, (blocks, 48, 128), 2) < 64
    out_ref[...] = jnp.where(left, total[:, :48], total[:, 48:]).astype(BF16)


def project(keep, other, mine, theirs):
    block = 8
    weights = pl.BlockSpec((block, 96, 128), lambda i: (i, 0, 0))
    tokens = pl.BlockSpec((192, 128), lambda i: (0, 0))
    return pl.pallas_call(
        project_kernel,
        grid=(NX * NZ // block,),
        in_specs=[weights, weights, tokens, tokens],
        out_specs=pl.BlockSpec((block, 48, 128), lambda i: (i, 0, 0)),
        out_shape=shape((NX * NZ, 48, 128)),
        cost_estimate=cost(2 * 3072 * 256 * 128, 2 * MIB),
        compiler_params=params(),
        name="project",
    )(keep, other, mine, theirs)


def project_rest_kernel(where_ref, keep_ref, other_ref, mine_ref, theirs_ref, after_ref, *out_refs):
    for far, out_ref in enumerate(out_refs):
        start = lax.rem(where_ref[1] + far, NX) * NZ
        total = nt_dot(keep_ref[pl.ds(start, NZ)].reshape(NZ * 96, 128), mine_ref[64:])
        total += nt_dot(other_ref[pl.ds(start, NZ)].reshape(NZ * 96, 128), theirs_ref[64:])
        out_ref[...] = total.astype(BF16).reshape(NZ, 96, 128)


def project_rest(where, keep, other, mine, theirs, after):
    return pl.pallas_call(
        project_rest_kernel,
        in_specs=[smem_spec()] + [vmem_spec()] * 4 + [any_spec()],
        out_specs=[vmem_spec()] * NX,
        out_shape=[shape((NZ, 96, 128))] * NX,
        cost_estimate=cost(2 * 3072 * 256 * 128, 3 * MIB),
        compiler_params=params(),
        name="project_rest",
    )(where, keep, other, mine, theirs, after)


def add_rest_kernel(*refs):
    in_refs, out_ref = refs[:-1], refs[-1]
    blank = jnp.zeros((32, 128), F32)
    for block in range(NZ):
        total = sum(in_ref[block].astype(F32) for in_ref in in_refs)
        total = jnp.concatenate([total, blank], 0).T
        out_ref[:, block] = total.astype(BF16).reshape(4, 32, 128)


def add_rest(parts):
    return pl.pallas_call(
        add_rest_kernel,
        in_specs=[vmem_spec()] * NX,
        out_specs=vmem_spec(),
        out_shape=shape((4, NZ, 32, 128)),
        cost_estimate=cost(MIB, MIB),
        compiler_params=params(),
        name="add_rest",
    )(*parts)


def residual_kernel(in_ref, hidden_ref, one_ref, two_ref, three_ref, send_ref):
    routed = (jnp.sum(in_ref[...].astype(F32), 0) + hidden_ref[...]).astype(BF16)
    for copy in range(send_ref.shape[0]):
        send_ref[copy] = routed


def routed_residual(parts, hidden, *after):
    return pl.pallas_call(
        residual_kernel,
        in_specs=[vmem_spec()] * 2 + [any_spec()] * 3,
        out_specs=vmem_spec(),
        out_shape=shape((NX * NZ, 48, 128)),
        cost_estimate=cost(MIB, MIB),
        compiler_params=params(),
        name="routed_residual",
    )(parts, hidden, *after)


def up_kernel(where_ref, mine_ref, theirs_ref, weight_ref, out_ref, total_ref, square_ref):
    index = pl.program_id(0)
    even = where_ref[0] == 0
    blocks = mine_ref.shape[0]
    mine, theirs = mine_ref[...], theirs_ref[...]
    first = jnp.where(even, mine, theirs)
    second = jnp.where(even, theirs, mine)
    left = lax.broadcasted_iota(jnp.int32, (48, 128), 1) < 64
    zero = jnp.zeros((48, 128), BF16)
    pieces = []
    for block in range(blocks):
        for part in (first, second):
            pieces += [jnp.where(left, part[block], zero), jnp.where(left, zero, part[block])]
    tokens = jnp.concatenate(pieces, 0)

    @pl.when(index == 0)
    def _():
        total_ref[...] = jnp.zeros_like(total_ref)
        square_ref[...] = jnp.zeros_like(square_ref)

    total_ref[...] += jnp.dot(weight_ref[...], tokens, preferred_element_type=F32)
    wide = tokens.astype(F32)
    square_ref[...] += jnp.sum((wide * wide).reshape(-1, 8, 128), 0)

    @pl.when(index == pl.num_programs(0) - 1)
    def _():
        total, square = total_ref[...], jnp.sum(square_ref[...], 0, keepdims=True)
        total = total[:, :64] + total[:, 64:]
        square = square[:, :64] + square[:, 64:]
        total = total * lax.rsqrt(square / 6144.0 + EPSILON_NORM)
        half = total.shape[0] // 2
        out_ref[...] = (silu(total[:half]) * total[half:]).astype(BF16)


def up_project(where, mine, theirs, weight):
    rows, width = weight.shape
    steps = 4
    tokens = pl.BlockSpec((32 // steps, 48, 128), lambda i: (i, 0, 0))
    return pl.pallas_call(
        up_kernel,
        grid=(steps,),
        in_specs=[smem_spec(), tokens, tokens, pl.BlockSpec((rows, width // steps), lambda i: (0, i))],
        out_specs=pl.BlockSpec((rows // 2, 64), lambda i: (0, 0)),
        out_shape=shape((rows // 2, 64)),
        scratch_shapes=[pltpu.VMEM((rows, 128), F32), pltpu.VMEM((8, 128), F32)],
        cost_estimate=cost(2 * 288 * 6144 * 128, 5 * MIB),
        compiler_params=params(),
        name="up_project",
    )(where, mine, theirs, in_hbm(weight))


def down_kernel(mine_ref, theirs_ref, keep_ref, other_ref, after_ref, out_ref):
    total = tn_dot(mine_ref[...], keep_ref[...]) + tn_dot(theirs_ref[...], other_ref[...])
    total = total.astype(BF16)
    for block in range(NZ):
        out_ref[0, block] = total[:, block * 128 : block * 128 + 128].reshape(4, 16, 128)


def down_project(mine, theirs, keep, other, after):
    hidden = mine.shape[0]
    tokens = pl.BlockSpec((hidden, 64), lambda i: (0, 0))
    weights = pl.BlockSpec((hidden, NZ * 128), lambda i: (0, i))
    return pl.pallas_call(
        down_kernel,
        grid=(NX,),
        in_specs=[tokens, tokens, weights, weights, any_spec()],
        out_specs=pl.BlockSpec((1, NZ, 4, 16, 128), lambda i: (i, 0, 0, 0, 0)),
        out_shape=shape((NX, NZ, 4, 16, 128)),
        cost_estimate=cost(2 * 288 * 4096 * 64, 3 * MIB),
        compiler_params=params(),
        name="down_project",
    )(mine, theirs, keep, other, after)


def merge_kernel(parts_ref, rest_ref, out_ref):
    out_ref[:, :, :32] = rest_ref[...]
    for block in range(NZ):
        out_ref[:, block, 32:] = jnp.sum(parts_ref[:, block].astype(F32), 0).astype(BF16)


def merge(parts, rest):
    return pl.pallas_call(
        merge_kernel,
        in_specs=[vmem_spec()] * 2,
        out_specs=vmem_spec(),
        out_shape=shape((4, NZ, 48, 128)),
        cost_estimate=cost(MIB, MIB),
        compiler_params=params(),
        name="merge",
    )(parts, rest)


def combine_kernel(parts_ref, place_ref, weight_ref, hidden_ref, out_ref):
    parts = jnp.sum(parts_ref[...].astype(F32), 1)
    residual = hidden_ref[...].astype(F32) + parts[:, :32].reshape(128, 128)
    result = parts[:, 32:].astype(BF16).reshape(64, 128)
    fetched = jnp.dot(place_ref[:, :64], result, preferred_element_type=F32)
    out_ref[...] = (residual + weight_ref[...] * fetched)[:, :96].astype(BF16)


def combine(parts, place, weight, hidden):
    return pl.pallas_call(
        combine_kernel,
        in_specs=[vmem_spec()] * 4,
        out_specs=vmem_spec(),
        out_shape=shape((128, 96)),
        cost_estimate=cost(MIB, MIB),
        compiler_params=params(),
        name="combine",
    )(parts, place, weight, hidden)


def swap(value):
    return lax.ppermute(value, "core", [(0, 1), (1, 0)])


def shifted(blocks, axis):
    count = len(blocks)
    return [blocks[0]] + [
        lax.ppermute(blocks[far], axis, [(i, (i + far) % count) for i in range(count)]) for far in range(1, count)
    ]


def per_device(
    unfinished, states, qkv_rows, decay_rate, out_weight, hidden_in, routes, route_weight, expert_up, expert_down
):
    where = jnp.stack([lax.axis_index("core").astype(jnp.int32), lax.axis_index("x").astype(jnp.int32)])

    with jax.named_scope("attention"):
        local = attend(states[0], qkv_rows[0].transpose(0, 2, 1, 3))
        parts = lax.all_to_all(local, HEAD, 0, 0, tiled=True)
    with jax.named_scope("weights"):
        keep_out, other_out = split_out(where, out_weight, swap(out_weight), local)
    with jax.named_scope("routing"):
        hidden = jnp.pad(hidden_in.transpose(1, 2, 0).reshape(128, 96), ((0, 0), (0, 32)))
        slots = jnp.repeat(unfinished, 4)[:, None]
        place, weight, facts = route(routes.reshape(128, 2), route_weight.reshape(128, 2), hidden, slots)
    with jax.named_scope("heads"):
        head_out = decay_heads(decay_rate, parts, facts, keep_out)
        head_rows = lax.all_to_all(head_out, "dp", 0, 0, tiled=True)
        mine, routed_hidden = select(head_rows.reshape(-1, 128))
        theirs = swap(mine)
    with jax.named_scope("projection"):
        partial = project(keep_out, other_out, mine, theirs)
        summed = lax.all_to_all(partial, ("x", "z"), 0, 0, tiled=True)
        keep_down, other_down = split_down(where, expert_down[0], swap(expert_down[0]), partial)
        rest = project_rest(where, keep_out, other_out, mine, theirs, partial)
        rest = shifted(rest, "x")
        routed = routed_residual(summed, routed_hidden, rest[1], rest[3], keep_down)
    with jax.named_scope("expert"):
        features = lax.all_to_all(routed, ("x", "z"), 0, 0, tiled=True)
        up = expert_up[0].transpose(1, 2, 0).reshape(288, 6144)
        expert_hidden = up_project(where, features, swap(features), up)
        results = down_project(expert_hidden, swap(expert_hidden), keep_down, other_down, rest[2])
        rest = add_rest(rest)
        over_x = lax.all_to_all(results, "x", 0, 0, tiled=True)
        merged = merge(over_x, rest).reshape(32, 48, 128)
        returned = lax.all_to_all(merged, ("dp", "z"), 0, 0, tiled=True)
    with jax.named_scope("output"):
        mixed = combine(returned.reshape(4, NZ, 48, 128), place, weight, hidden)
        return mixed.reshape(32, 4, 96).transpose(2, 0, 1)


def solution(mesh):
    grid = Mesh(mesh.devices.reshape(mesh.shape["dp"], NX, NZ, NC), EVERY)
    return jax.shard_map(
        per_device,
        mesh=grid,
        in_specs=(
            P("dp"),
            P(EVERY, None, None, None),
            P(EVERY, None, None, None, None),
            P(HEAD),
            P(HEAD, None),
            P(HEAD, "dp", None),
            P("dp", None, None),
            P("dp", None, None),
            P("dp", None, None, HEAD),
            P("dp", HEAD, None),
        ),
        out_specs=P(HEAD, "dp", None),
        check_vma=False,
    )
```

```python
import functools

import jax
import jax.numpy as jnp
from jax import lax
from jax.experimental import pallas as pl
from jax.experimental.pallas import tpu as pltpu
from jax.sharding import Mesh, PartitionSpec as P

EPSILON_HEAD = 1e-06
EPSILON_NORM = 1e-05
BF16, F32 = jnp.bfloat16, jnp.float32
NX, NZ, NC = 4, 8, 2
EVERY = ("dp", "x", "z", "core")
HEAD = ("x", "z", "core")
MIB = 1 << 20


def vmem_spec():
    return pl.BlockSpec(memory_space=pltpu.VMEM)


def smem_spec():
    return pl.BlockSpec(memory_space=pltpu.SMEM)


def any_spec():
    return pl.BlockSpec(memory_space=pl.ANY)


def in_hbm(value):
    return pltpu.with_memory_space_constraint(value, pltpu.HBM)


def params(mib=12):
    return pltpu.CompilerParams(vmem_limit_bytes=mib * MIB)


def cost(flops, size):
    return pl.CostEstimate(flops=flops, bytes_accessed=size, transcendentals=0)


def shape(dims, dtype=BF16):
    return jax.ShapeDtypeStruct(dims, dtype)


def nt_dot(left, right):
    return lax.dot_general(left, right, (((1,), (1,)), ((), ())), preferred_element_type=F32)


def tn_dot(left, right):
    return lax.dot_general(left, right, (((0,), (0,)), ((), ())), preferred_element_type=F32)


def silu(value):
    return value / (1.0 + jnp.exp(-value))


def one_hot(mask):
    return mask.astype(F32).astype(BF16)


def attend_kernel(state_ref, input_ref, out_ref):
    heads = state_ref.shape[0]
    query = silu(input_ref[:, 0].astype(F32))
    key = silu(input_ref[:, 1].astype(F32))
    high = query.astype(BF16).astype(F32)
    both = jnp.concatenate([high, query - high], 1).astype(BF16)
    for head in range(heads):
        base = jnp.dot(both[head], state_ref[head], preferred_element_type=F32)
        out_ref[head, 0] = (base[:4] + base[4:]).astype(BF16)
    out_ref[:, 1] = input_ref[:, 2]
    lane = lax.broadcasted_iota(jnp.int32, query.shape, 2)
    cross = jnp.zeros(query.shape, F32)
    for source in range(4):
        weight = jnp.sum(query * key[:, source : source + 1], -1, keepdims=True)
        whole = weight.astype(BF16).astype(F32)
        cross = jnp.where(lane == source, whole, cross)
        cross = jnp.where(lane == source + 4, weight - whole, cross)
    out_ref[:, 2] = cross.astype(BF16)


def attend(states, inputs):
    heads, block = states.shape[0], 32
    return pl.pallas_call(
        attend_kernel,
        grid=(heads // block,),
        in_specs=[
            pl.BlockSpec((block, 128, 128), lambda i: (i, 0, 0)),
            pl.BlockSpec((block, 3, 4, 128), lambda i: (i, 0, 0, 0)),
        ],
        out_specs=pl.BlockSpec((block, 3, 4, 128), lambda i: (i, 0, 0, 0)),
        out_shape=shape((heads, 3, 4, 128)),
        cost_estimate=cost(2 * 8 * 64 * 128 * 128, 3 * MIB),
        compiler_params=params(),
        name="attend",
    )(in_hbm(states), in_hbm(inputs))


def decay_kernel(where_ref, rate_ref, parts_ref, facts_ref, after_ref, *out_refs):
    slots = parts_ref.shape[0]
    rate = jnp.full((4, 128), rate_ref[0], F32)
    step = lax.broadcasted_iota(jnp.int32, (4, 128), 0).astype(F32)
    value = parts_ref[:, 1].astype(F32)
    cross = parts_ref[:, 2].astype(F32)
    cross += pltpu.roll(cross, 124, 2)
    attn = jnp.exp(-rate * (step + 1.0)) * parts_ref[:, 0].astype(F32)
    for source in range(4):
        factor = jnp.where(step >= source, jnp.exp(-rate * jnp.maximum(step - source, 0.0)), 0.0)
        attn += (factor * cross[:, :, source : source + 1]) * value[:, source : source + 1]
    scaled = attn * lax.rsqrt(jnp.mean(attn * attn, -1, keepdims=True) + EPSILON_HEAD)
    scaled = scaled.astype(BF16)
    for far, out_ref in enumerate(out_refs):
        out_ref[:slots] = scaled
        out_ref[slots:] = facts_ref[lax.rem(where_ref[2] + far, 4)]


def decay_heads(where, rate, parts, facts, after):
    slots = parts.shape[0]
    return pl.pallas_call(
        decay_kernel,
        in_specs=[smem_spec(), smem_spec(), vmem_spec(), vmem_spec(), any_spec()],
        out_specs=[vmem_spec()] * 4,
        out_shape=[shape((slots + 4, 4, 128))] * 4,
        cost_estimate=cost(4 * MIB, MIB),
        compiler_params=params(),
        name="decay_heads",
    )(where, rate, parts, facts, after)


def route_kernel(pair_ref, weight_ref, hidden_ref, row_ref, place_ref, factor_ref, out_ref):
    pair = pair_ref[...]
    expert = jnp.min(pair, 1, keepdims=True)
    factor_ref[...] = jnp.sum(jnp.where(pair < 4, weight_ref[...], 0.0), 1, keepdims=True)
    token = lax.broadcasted_iota(jnp.int32, (128, 128), 0)
    lane = lax.broadcasted_iota(jnp.int32, (128, 128), 1)
    named = (lane == expert).astype(F32)
    ranks = jnp.dot(one_hot(token > lane), named.astype(BF16), preferred_element_type=F32)
    rank = jnp.sum(ranks * named, 1, keepdims=True).astype(jnp.int32)
    position = jnp.where(expert < 4, expert * 16 + rank, -1)
    place = one_hot(lane == position)
    place_ref[...] = place
    row = row_ref[...].astype(F32)
    facts = hidden_ref[...].astype(F32)
    facts = jnp.where(lane == 96, row, jnp.where(lane == 97, (token % 4).astype(F32), facts))
    slots = jnp.where(lane == 98, row, 0.0)
    quarter = one_hot((token % 16 < 8) & (lane == (token // 16 * 8 + token % 16) * 4))
    packed = tn_dot(place, facts.astype(BF16)) + jnp.dot(quarter, slots.astype(BF16), preferred_element_type=F32)
    out_ref[...] = packed[:64].reshape(4, 4, 4, 128).astype(BF16)


def route(pair, weight, hidden, row):
    return pl.pallas_call(
        route_kernel,
        in_specs=[vmem_spec()] * 4,
        out_specs=[vmem_spec()] * 3,
        out_shape=[shape((128, 128)), shape((128, 1), F32), shape((4, 4, 4, 128))],
        cost_estimate=cost(8 * MIB, MIB // 2),
        compiler_params=params(),
        name="route",
    )(pair, weight, hidden, row)


def select_kernel(where_ref, *refs):
    in_refs, (out_ref, hidden_ref, held_ref) = refs[:4], refs[4:]
    span = held_ref.shape[1]
    steps = span - 16
    for far, in_ref in enumerate(in_refs):
        held_ref[lax.rem(where_ref[2] + (4 - far), 4)] = in_ref[...]
    rows = held_ref[...].reshape(4 * span, 128)
    facts = held_ref[:, steps:].reshape(64, 128)
    held = facts.astype(F32)
    token = lax.broadcasted_iota(jnp.int32, (128, 64), 0)
    source = lax.broadcasted_iota(jnp.int32, (128, 64), 1)
    spread = one_hot(source == token // 32 * 16 + token % 32 // 4)
    rest = jnp.dot(spread, facts, preferred_element_type=F32)
    step = (lax.broadcasted_iota(jnp.int32, (128, 1), 0) % 4).astype(F32)
    row = jnp.concatenate([held[:, 96:97], rest[:, 98:99]], 0)
    step = jnp.concatenate([held[:, 97:98], step], 0)
    row = (row * 4.0 + step).astype(jnp.int32)
    row = row // steps * span + row % steps
    lane = lax.broadcasted_iota(jnp.int32, (192, 4 * span), 1)
    out_ref[...] = jnp.dot(one_hot(lane == row), rows, preferred_element_type=F32).astype(BF16)
    turned = jnp.concatenate([held, held], 0).T
    left = lax.broadcasted_iota(jnp.int32, (48, 128), 1) < 64
    hidden_ref[...] = jnp.where(left, turned[:48], turned[48:96])


def select(where, parts):
    return pl.pallas_call(
        select_kernel,
        in_specs=[smem_spec()] + [vmem_spec()] * 4,
        out_specs=[vmem_spec()] * 2,
        out_shape=[shape((192, 128)), shape((48, 128), F32)],
        scratch_shapes=[pltpu.VMEM((4,) + parts[0].shape, BF16)],
        cost_estimate=cost(2 * 192 * 1088 * 128, MIB),
        compiler_params=params(),
        name="select",
    )(where, *parts)


def split_out_kernel(where_ref, mine_ref, theirs_ref, after_ref, *out_refs):
    core = where_ref[0]
    row = lax.broadcasted_iota(jnp.int32, (192, 384), 0)
    lane = lax.broadcasted_iota(jnp.int32, (192, 384), 1)
    pick = one_hot(lane == row // 96 * 192 + row % 96 + core * 96)
    for part in range(8):
        for weight_ref, out_ref in zip((mine_ref, theirs_ref), out_refs):
            weight = weight_ref[:, part * 384 : part * 384 + 384]
            out_ref[2 * part : 2 * part + 2] = nt_dot(pick, weight).astype(BF16).reshape(2, 96, 128)


def split_out(where, mine, theirs, after):
    return pl.pallas_call(
        split_out_kernel,
        grid=(2,),
        in_specs=[smem_spec()] + [pl.BlockSpec((128, 3072), lambda i: (0, i))] * 2 + [any_spec()],
        out_specs=[pl.BlockSpec((16, 96, 128), lambda i: (i, 0, 0))] * 2,
        out_shape=[shape((NX * NZ, 96, 128))] * 2,
        cost_estimate=cost(2 * 16 * 384 * 384 * 128, 3 * MIB),
        compiler_params=params(),
        name="split_out",
    )(where, mine, in_hbm(theirs), after)


def split_down_kernel(where_ref, mine_ref, theirs_ref, after_ref, *out_refs):
    core = where_ref[0]
    row = lax.broadcasted_iota(jnp.int32, (384, 256), 0)
    lane = lax.broadcasted_iota(jnp.int32, (384, 256), 1)
    pick = one_hot((row == lane // 128 * 192 + lane % 128 + core * 96) & (lane % 128 < 96))
    for part in range(4):
        for weight_ref, out_ref in zip((mine_ref, theirs_ref), out_refs):
            weight = weight_ref[:, part * 384 : part * 384 + 384]
            total = jnp.dot(weight, pick, preferred_element_type=F32)
            out_ref[:, part * 256 : part * 256 + 256] = total.astype(BF16)


def split_down(where, mine, theirs, after):
    hidden = mine.shape[0]
    weights = pl.BlockSpec((hidden, 1536), lambda i, where: (0, lax.rem(where[1] + i, NX)))
    return pl.pallas_call(
        split_down_kernel,
        grid_spec=pltpu.PrefetchScalarGridSpec(
            num_scalar_prefetch=1,
            grid=(NX,),
            in_specs=[weights, weights, any_spec()],
            out_specs=[pl.BlockSpec((hidden, NZ * 128), lambda i, where: (0, i))] * 2,
        ),
        out_shape=[shape((hidden, NX * NZ * 128))] * 2,
        cost_estimate=cost(2 * 16 * 384 * 512 * 144, 4 * MIB),
        compiler_params=params(),
        name="split_down",
    )(where, mine, in_hbm(theirs), after)


def project_kernel(keep_ref, other_ref, mine_ref, theirs_ref, out_ref):
    blocks = keep_ref.shape[0]
    mine, theirs = mine_ref[:64], theirs_ref[:64]
    total = nt_dot(keep_ref[...].reshape(blocks * 96, 128), jnp.concatenate([mine, mine], 0))
    total += nt_dot(other_ref[...].reshape(blocks * 96, 128), jnp.concatenate([theirs, theirs], 0))
    total = total.reshape(blocks, 96, 128)
    left = lax.broadcasted_iota(jnp.int32, (blocks, 48, 128), 2) < 64
    total = jnp.where(left, total[:, :48], total[:, 48:]).astype(BF16)
    for column in range(blocks // NZ):
        out_ref[:, column] = total[column * NZ : (column + 1) * NZ]


def project(keep, other, mine, theirs):
    block = 16
    weights = pl.BlockSpec((block, 96, 128), lambda i: (i, 0, 0))
    tokens = pl.BlockSpec((192, 128), lambda i: (0, 0))
    return pl.pallas_call(
        project_kernel,
        grid=(NX * NZ // block,),
        in_specs=[weights, weights, tokens, tokens],
        out_specs=pl.BlockSpec((NZ, block // NZ, 48, 128), lambda i: (0, i, 0, 0)),
        out_shape=shape((NZ, NX, 48, 128)),
        cost_estimate=cost(2 * 3072 * 256 * 128, 2 * MIB),
        compiler_params=params(),
        name="project",
    )(keep, other, mine, theirs)


def project_rest_kernel(where_ref, keep_ref, other_ref, mine_ref, theirs_ref, after_ref, *out_refs):
    for far, out_ref in enumerate(out_refs):
        start = lax.rem(where_ref[1] + far, NX) * NZ
        total = nt_dot(keep_ref[pl.ds(start, NZ)].reshape(NZ * 96, 128), mine_ref[64:])
        total += nt_dot(other_ref[pl.ds(start, NZ)].reshape(NZ * 96, 128), theirs_ref[64:])
        out_ref[...] = total.astype(BF16).reshape(NZ, 96, 128)


def project_rest(where, keep, other, mine, theirs, after):
    return pl.pallas_call(
        project_rest_kernel,
        in_specs=[smem_spec()] + [vmem_spec()] * 4 + [any_spec()],
        out_specs=[vmem_spec()] * NX,
        out_shape=[shape((NZ, 96, 128))] * NX,
        cost_estimate=cost(2 * 3072 * 256 * 128, 3 * MIB),
        compiler_params=params(),
        name="project_rest",
    )(where, keep, other, mine, theirs, after)


def add_rest_kernel(*refs):
    in_refs, out_ref = refs[:-1], refs[-1]
    blank = jnp.zeros((32, 128), F32)
    for block in range(NZ):
        total = sum(in_ref[block].astype(F32) for in_ref in in_refs)
        total = jnp.concatenate([total, blank], 0).T
        out_ref[:, block] = total.astype(BF16).reshape(4, 32, 128)


def add_rest(parts):
    return pl.pallas_call(
        add_rest_kernel,
        in_specs=[vmem_spec()] * NX,
        out_specs=vmem_spec(),
        out_shape=shape((4, NZ, 32, 128)),
        cost_estimate=cost(MIB, MIB),
        compiler_params=params(),
        name="add_rest",
    )(*parts)


def residual_kernel(in_ref, hidden_ref, one_ref, two_ref, three_ref, send_ref):
    routed = (jnp.sum(in_ref[...].astype(F32), 0) + hidden_ref[...]).astype(BF16)
    for copy in range(send_ref.shape[0]):
        send_ref[copy] = routed


def routed_residual(parts, hidden, *after):
    return pl.pallas_call(
        residual_kernel,
        in_specs=[vmem_spec()] * 2 + [any_spec()] * 3,
        out_specs=vmem_spec(),
        out_shape=shape((NX * NZ, 48, 128)),
        cost_estimate=cost(MIB, MIB),
        compiler_params=params(),
        name="routed_residual",
    )(parts, hidden, *after)


def start_copies(pairs, sems):
    copies = [pltpu.make_async_copy(source, target, sems.at[i]) for i, (source, target) in enumerate(pairs)]
    for copy in copies:
        copy.start()
    return copies


def up_kernel(where_ref, mine_ref, theirs_ref, weight_ref, out_ref, held_ref, sems):
    step = 4
    parts = range(0, mine_ref.shape[0], step)
    span = step * 192
    copies = start_copies(
        [(weight_ref.at[:, pl.ds(start * 192, span)], held_ref.at[index]) for index, start in enumerate(parts)], sems
    )
    even = where_ref[0] == 0
    left = lax.broadcasted_iota(jnp.int32, (48, 128), 1) < 64
    zero = jnp.zeros((48, 128), BF16)
    total = jnp.zeros((weight_ref.shape[0], 128), F32)
    square = jnp.zeros((8, 128), F32)
    for index, start in enumerate(parts):
        pieces = []
        for block in range(start, start + step):
            place = block % NZ * NX + block // NZ
            mine, theirs = mine_ref[place], theirs_ref[place]
            for part in (jnp.where(even, mine, theirs), jnp.where(even, theirs, mine)):
                pieces += [jnp.where(left, part, zero), jnp.where(left, zero, part)]
                wide = part.astype(F32)
                square += jnp.sum((wide * wide).reshape(6, 8, 128), 0)
        tokens = jnp.concatenate(pieces, 0)
        copies[index].wait()
        total += jnp.dot(held_ref[index], tokens, preferred_element_type=F32)
    square = jnp.sum(square, 0, keepdims=True)
    total = total[:, :64] + total[:, 64:]
    square = square[:, :64] + square[:, 64:]
    total = total * lax.rsqrt(square / 6144.0 + EPSILON_NORM)
    half = total.shape[0] // 2
    out_ref[...] = (silu(total[:half]) * total[half:]).astype(BF16)


def up_project(where, mine, theirs, weight):
    rows, width = weight.shape
    return pl.pallas_call(
        up_kernel,
        in_specs=[smem_spec(), vmem_spec(), vmem_spec(), any_spec()],
        out_specs=vmem_spec(),
        out_shape=shape((rows // 2, 64)),
        scratch_shapes=[pltpu.VMEM((8, rows, width // 8), BF16), pltpu.SemaphoreType.DMA((8,))],
        cost_estimate=cost(2 * 288 * 6144 * 128, 5 * MIB),
        compiler_params=params(),
        name="up_project",
    )(where, mine, theirs, in_hbm(weight))


def down_kernel(mine_ref, theirs_ref, keep_ref, other_ref, *out_refs):
    total = tn_dot(mine_ref[...], keep_ref[...]) + tn_dot(theirs_ref[...], other_ref[...])
    total = total.astype(BF16)
    half = NX // 2
    for step in range(2):

        @pl.when(pl.program_id(0) == step)
        def _():
            for column in range(half):
                for block in range(NZ):
                    start = (column * NZ + block) * 128
                    out_refs[step * half + column][block] = total[:, start : start + 128].reshape(4, 16, 128)


def down_project(mine, theirs, keep, other):
    hidden = mine.shape[0]
    tokens = pl.BlockSpec((hidden, 64), lambda i: (0, 0))
    weights = pl.BlockSpec((hidden, NX * NZ * 64), lambda i: (0, i))
    return pl.pallas_call(
        down_kernel,
        grid=(2,),
        in_specs=[tokens, tokens, weights, weights],
        out_specs=[pl.BlockSpec((NZ, 4, 16, 128), lambda i: (0, 0, 0, 0))] * NX,
        out_shape=[shape((NZ, 4, 16, 128))] * NX,
        cost_estimate=cost(2 * 288 * 4096 * 64, 3 * MIB),
        compiler_params=params(16),
        name="down_project",
    )(mine, theirs, keep, other)


def merge_kernel(rest_ref, *refs):
    in_refs, out_ref = refs[:-1], refs[-1]
    out_ref[:, :, :32] = rest_ref[...]
    for block in range(NZ):
        out_ref[:, block, 32:] = sum(in_ref[block].astype(F32) for in_ref in in_refs).astype(BF16)


def merge(rest, parts):
    return pl.pallas_call(
        merge_kernel,
        in_specs=[vmem_spec()] * (1 + NX),
        out_specs=vmem_spec(),
        out_shape=shape((4, NZ, 48, 128)),
        cost_estimate=cost(MIB, MIB),
        compiler_params=params(),
        name="merge",
    )(rest, *parts)


def combine_kernel(parts_ref, place_ref, weight_ref, hidden_ref, out_ref):
    parts = jnp.sum(parts_ref[...].astype(F32), 1)
    residual = hidden_ref[...].astype(F32) + parts[:, :32].reshape(128, 128)
    result = parts[:, 32:].astype(BF16).reshape(64, 128)
    fetched = jnp.dot(place_ref[:, :64], result, preferred_element_type=F32)
    out_ref[...] = (residual + weight_ref[...] * fetched)[:, :96].astype(BF16)


def combine(parts, place, weight, hidden):
    return pl.pallas_call(
        combine_kernel,
        in_specs=[vmem_spec()] * 4,
        out_specs=vmem_spec(),
        out_shape=shape((128, 96)),
        cost_estimate=cost(MIB, MIB),
        compiler_params=params(),
        name="combine",
    )(parts, place, weight, hidden)


def gate_kernel(value_ref, after_ref, out_ref):
    pass


def gate(value, after):
    return pl.pallas_call(
        gate_kernel,
        in_specs=[pl.BlockSpec(memory_space=pltpu.VMEM), any_spec()],
        out_specs=pl.BlockSpec(memory_space=pltpu.VMEM),
        out_shape=jax.ShapeDtypeStruct(value.shape, value.dtype),
        input_output_aliases={0: 0},
        compiler_params=params(1),
        name="gate",
    )(value, after)


def swap(value):
    return lax.ppermute(value, "core", [(0, 1), (1, 0)])


def shifted(blocks, axis):
    count = len(blocks)
    return [blocks[0]] + [
        lax.ppermute(blocks[far], axis, [(i, (i + far) % count) for i in range(count)]) for far in range(1, count)
    ]


def per_device(
    unfinished, states, qkv_rows, decay_rate, out_weight, hidden_in, routes, route_weight, expert_up, expert_down
):
    where = jnp.stack([lax.axis_index(axis).astype(jnp.int32) for axis in ("core", "x", "dp")])

    with jax.named_scope("attention"):
        local = attend(states[0], qkv_rows[0].transpose(0, 2, 1, 3))
        parts = lax.all_to_all(local, HEAD, 0, 0, tiled=True)
    with jax.named_scope("weights"):
        keep_out, other_out = split_out(where, out_weight, swap(out_weight), local)
    with jax.named_scope("routing"):
        hidden = jnp.pad(hidden_in.transpose(1, 2, 0).reshape(128, 96), ((0, 0), (0, 32)))
        slots = jnp.repeat(unfinished, 4)[:, None]
        place, weight, facts = route(routes.reshape(128, 2), route_weight.reshape(128, 2), hidden, slots)
    with jax.named_scope("heads"):
        head_out = decay_heads(where, decay_rate, parts, facts, keep_out)
        head_rows = [rows.reshape(-1, 128) for rows in shifted(head_out, "dp")]
        mine, routed_hidden = select(where, head_rows)
        theirs = swap(mine)
    with jax.named_scope("projection"):
        partial = project(keep_out, other_out, mine, theirs)
        summed = lax.all_to_all(partial.reshape(NZ * NX, 48, 128), ("z", "x"), 0, 0, tiled=True)
        keep_down, other_down = split_down(where, expert_down[0], swap(expert_down[0]), partial)
        rest = project_rest(where, keep_out, other_out, mine, theirs, partial)
        rest = shifted(rest, "x")
        routed = routed_residual(summed, routed_hidden, rest[1], rest[3], keep_down)
    with jax.named_scope("expert"):
        features = gate(lax.all_to_all(routed, ("z", "x"), 0, 0, tiled=True), rest[2])
        up = expert_up[0].transpose(1, 2, 0).reshape(288, 6144)
        expert_hidden = up_project(where, features, swap(features), up)
        results = down_project(expert_hidden, swap(expert_hidden), keep_down, other_down)
        rest = add_rest(rest)
        merged = merge(rest, shifted(results, "x")).reshape(32, 48, 128)
        returned = lax.all_to_all(merged, ("dp", "z"), 0, 0, tiled=True)
    with jax.named_scope("output"):
        mixed = combine(returned.reshape(4, NZ, 48, 128), place, weight, hidden)
        return mixed.reshape(32, 4, 96).transpose(2, 0, 1)


def solution(mesh):
    grid = Mesh(mesh.devices.reshape(mesh.shape["dp"], NX, NZ, NC), EVERY)
    return jax.shard_map(
        per_device,
        mesh=grid,
        in_specs=(
            P("dp"),
            P(EVERY, None, None, None),
            P(EVERY, None, None, None, None),
            P(HEAD),
            P(HEAD, None),
            P(HEAD, "dp", None),
            P("dp", None, None),
            P("dp", None, None),
            P("dp", None, None, HEAD),
            P("dp", HEAD, None),
        ),
        out_specs=P(HEAD, "dp", None),
        check_vma=False,
    )
```

```python
import functools

import jax
import jax.numpy as jnp
from jax import lax
from jax.experimental import pallas as pl
from jax.experimental.pallas import tpu as pltpu
from jax.sharding import Mesh, PartitionSpec as P

EPSILON_HEAD = 1e-06
EPSILON_NORM = 1e-05
BF16, F32 = jnp.bfloat16, jnp.float32
NX, NZ, NC = 4, 8, 2
EVERY = ("dp", "x", "z", "core")
HEAD = ("x", "z", "core")
MIB = 1 << 20


def vmem_spec():
    return pl.BlockSpec(memory_space=pltpu.VMEM)


def smem_spec():
    return pl.BlockSpec(memory_space=pltpu.SMEM)


def any_spec():
    return pl.BlockSpec(memory_space=pl.ANY)


def in_hbm(value):
    return pltpu.with_memory_space_constraint(value, pltpu.HBM)


def params(mib=12):
    return pltpu.CompilerParams(vmem_limit_bytes=mib * MIB)


def cost(flops, size):
    return pl.CostEstimate(flops=flops, bytes_accessed=size, transcendentals=0)


def shape(dims, dtype=BF16):
    return jax.ShapeDtypeStruct(dims, dtype)


def nt_dot(left, right):
    return lax.dot_general(left, right, (((1,), (1,)), ((), ())), preferred_element_type=F32)


def tn_dot(left, right):
    return lax.dot_general(left, right, (((0,), (0,)), ((), ())), preferred_element_type=F32)


def silu(value):
    return value / (1.0 + jnp.exp(-value))


def one_hot(mask):
    return mask.astype(F32).astype(BF16)


def attend_kernel(state_ref, input_ref, out_ref):
    heads = state_ref.shape[0]
    query = silu(input_ref[:, 0].astype(F32))
    key = silu(input_ref[:, 1].astype(F32))
    high = query.astype(BF16).astype(F32)
    both = jnp.concatenate([high, query - high], 1).astype(BF16)
    for head in range(heads):
        base = jnp.dot(both[head], state_ref[head], preferred_element_type=F32)
        out_ref[head, 0] = (base[:4] + base[4:]).astype(BF16)
    out_ref[:, 1] = input_ref[:, 2]
    lane = lax.broadcasted_iota(jnp.int32, query.shape, 2)
    cross = jnp.zeros(query.shape, F32)
    for source in range(4):
        weight = jnp.sum(query * key[:, source : source + 1], -1, keepdims=True)
        whole = weight.astype(BF16).astype(F32)
        cross = jnp.where(lane == source, whole, cross)
        cross = jnp.where(lane == source + 4, weight - whole, cross)
    out_ref[:, 2] = cross.astype(BF16)


def attend(states, inputs):
    heads, block = states.shape[0], 32
    return pl.pallas_call(
        attend_kernel,
        grid=(heads // block,),
        in_specs=[
            pl.BlockSpec((block, 128, 128), lambda i: (i, 0, 0)),
            pl.BlockSpec((block, 3, 4, 128), lambda i: (i, 0, 0, 0)),
        ],
        out_specs=pl.BlockSpec((block, 3, 4, 128), lambda i: (i, 0, 0, 0)),
        out_shape=shape((heads, 3, 4, 128)),
        cost_estimate=cost(2 * 8 * 64 * 128 * 128, 3 * MIB),
        compiler_params=params(),
        name="attend",
    )(in_hbm(states), in_hbm(inputs))


def decay_kernel(where_ref, rate_ref, parts_ref, facts_ref, after_ref, *out_refs):
    slots = parts_ref.shape[0]
    rate = jnp.full((4, 128), rate_ref[0], F32)
    step = lax.broadcasted_iota(jnp.int32, (4, 128), 0).astype(F32)
    value = parts_ref[:, 1].astype(F32)
    cross = parts_ref[:, 2].astype(F32)
    cross += pltpu.roll(cross, 124, 2)
    attn = jnp.exp(-rate * (step + 1.0)) * parts_ref[:, 0].astype(F32)
    for source in range(4):
        factor = jnp.where(step >= source, jnp.exp(-rate * jnp.maximum(step - source, 0.0)), 0.0)
        attn += (factor * cross[:, :, source : source + 1]) * value[:, source : source + 1]
    scaled = attn * lax.rsqrt(jnp.mean(attn * attn, -1, keepdims=True) + EPSILON_HEAD)
    scaled = scaled.astype(BF16)
    for far, out_ref in enumerate(out_refs):
        out_ref[:slots] = scaled
        out_ref[slots:] = facts_ref[lax.rem(where_ref[2] + far, 4)]


def decay_heads(where, rate, parts, facts, after):
    slots = parts.shape[0]
    return pl.pallas_call(
        decay_kernel,
        in_specs=[smem_spec(), smem_spec(), vmem_spec(), vmem_spec(), any_spec()],
        out_specs=[vmem_spec()] * 4,
        out_shape=[shape((slots + 4, 4, 128))] * 4,
        cost_estimate=cost(4 * MIB, MIB),
        compiler_params=params(),
        name="decay_heads",
    )(where, rate, parts, facts, after)


def route_kernel(pair_ref, weight_ref, hidden_ref, row_ref, place_ref, factor_ref, out_ref):
    pair = pair_ref[...]
    expert = jnp.min(pair, 1, keepdims=True)
    factor_ref[...] = jnp.sum(jnp.where(pair < 4, weight_ref[...], 0.0), 1, keepdims=True)
    token = lax.broadcasted_iota(jnp.int32, (128, 128), 0)
    lane = lax.broadcasted_iota(jnp.int32, (128, 128), 1)
    named = (lane == expert).astype(F32)
    ranks = jnp.dot(one_hot(token > lane), named.astype(BF16), preferred_element_type=F32)
    rank = jnp.sum(ranks * named, 1, keepdims=True).astype(jnp.int32)
    position = jnp.where(expert < 4, expert * 16 + rank, -1)
    place = one_hot(lane == position)
    place_ref[...] = place
    row = row_ref[...].astype(F32)
    facts = hidden_ref[...].astype(F32)
    facts = jnp.where(lane == 96, row, jnp.where(lane == 97, (token % 4).astype(F32), facts))
    slots = jnp.where(lane == 98, row, 0.0)
    quarter = one_hot((token % 16 < 8) & (lane == (token // 16 * 8 + token % 16) * 4))
    packed = tn_dot(place, facts.astype(BF16)) + jnp.dot(quarter, slots.astype(BF16), preferred_element_type=F32)
    out_ref[...] = packed[:64].reshape(4, 4, 4, 128).astype(BF16)


def route(pair, weight, hidden, row):
    return pl.pallas_call(
        route_kernel,
        in_specs=[vmem_spec()] * 4,
        out_specs=[vmem_spec()] * 3,
        out_shape=[shape((128, 128)), shape((128, 1), F32), shape((4, 4, 4, 128))],
        cost_estimate=cost(8 * MIB, MIB // 2),
        compiler_params=params(),
        name="route",
    )(pair, weight, hidden, row)


def select_kernel(where_ref, *refs):
    in_refs, (out_ref, hidden_ref, held_ref) = refs[:4], refs[4:]
    span = held_ref.shape[1]
    steps = span - 16
    for far, in_ref in enumerate(in_refs):
        held_ref[lax.rem(where_ref[2] + (4 - far), 4)] = in_ref[...]
    rows = held_ref[...].reshape(4 * span, 128)
    facts = held_ref[:, steps:].reshape(64, 128)
    held = facts.astype(F32)
    token = lax.broadcasted_iota(jnp.int32, (128, 64), 0)
    source = lax.broadcasted_iota(jnp.int32, (128, 64), 1)
    spread = one_hot(source == token // 32 * 16 + token % 32 // 4)
    rest = jnp.dot(spread, facts, preferred_element_type=F32)
    step = (lax.broadcasted_iota(jnp.int32, (128, 1), 0) % 4).astype(F32)
    row = jnp.concatenate([held[:, 96:97], rest[:, 98:99]], 0)
    step = jnp.concatenate([held[:, 97:98], step], 0)
    row = (row * 4.0 + step).astype(jnp.int32)
    row = row // steps * span + row % steps
    lane = lax.broadcasted_iota(jnp.int32, (192, 4 * span), 1)
    out_ref[...] = jnp.dot(one_hot(lane == row), rows, preferred_element_type=F32).astype(BF16)
    turned = jnp.concatenate([held, held], 0).T
    left = lax.broadcasted_iota(jnp.int32, (48, 128), 1) < 64
    hidden_ref[...] = jnp.where(left, turned[:48], turned[48:96])


def select(where, parts):
    return pl.pallas_call(
        select_kernel,
        in_specs=[smem_spec()] + [vmem_spec()] * 4,
        out_specs=[vmem_spec()] * 2,
        out_shape=[shape((192, 128)), shape((48, 128), F32)],
        scratch_shapes=[pltpu.VMEM((4,) + parts[0].shape, BF16)],
        cost_estimate=cost(2 * 192 * 1088 * 128, MIB),
        compiler_params=params(),
        name="select",
    )(where, *parts)


def split_out_kernel(where_ref, mine_ref, theirs_ref, after_ref, *out_refs):
    core = where_ref[0]
    row = lax.broadcasted_iota(jnp.int32, (192, 384), 0)
    lane = lax.broadcasted_iota(jnp.int32, (192, 384), 1)
    pick = one_hot(lane == row // 96 * 192 + row % 96 + core * 96)
    for part in range(8):
        for weight_ref, out_ref in zip((mine_ref, theirs_ref), out_refs):
            weight = weight_ref[:, part * 384 : part * 384 + 384]
            out_ref[2 * part : 2 * part + 2] = nt_dot(pick, weight).astype(BF16).reshape(2, 96, 128)


def split_out(where, mine, theirs, after):
    return pl.pallas_call(
        split_out_kernel,
        grid=(2,),
        in_specs=[smem_spec()] + [pl.BlockSpec((128, 3072), lambda i: (0, i))] * 2 + [any_spec()],
        out_specs=[pl.BlockSpec((16, 96, 128), lambda i: (i, 0, 0))] * 2,
        out_shape=[shape((NX * NZ, 96, 128))] * 2,
        cost_estimate=cost(2 * 16 * 384 * 384 * 128, 3 * MIB),
        compiler_params=params(),
        name="split_out",
    )(where, mine, in_hbm(theirs), after)


def own_blocks(core):
    row = lax.broadcasted_iota(jnp.int32, (768, 384), 0)
    lane = lax.broadcasted_iota(jnp.int32, (768, 384), 1)
    return one_hot(row == lane // 96 * 192 + lane % 96 + core * 96)


def split_down_kernel(where_ref, mine_ref, theirs_ref, after_ref, *out_refs):
    pick = own_blocks(where_ref[0])
    for part in range(2):
        for weight_ref, out_ref in zip((mine_ref, theirs_ref), out_refs):
            weight = weight_ref[:, part * 768 : part * 768 + 768]
            out_ref[:, part * 384 : part * 384 + 384] = jnp.dot(weight, pick, preferred_element_type=F32).astype(BF16)


def split_down(where, mine, theirs, after):
    hidden = mine.shape[0]
    weights = pl.BlockSpec((hidden, 1536), lambda i, where: (0, lax.rem(where[1] + i, NX)))
    return pl.pallas_call(
        split_down_kernel,
        grid_spec=pltpu.PrefetchScalarGridSpec(
            num_scalar_prefetch=1,
            grid=(NX,),
            in_specs=[weights, weights, any_spec()],
            out_specs=[pl.BlockSpec((hidden, NZ * 96), lambda i, where: (0, i))] * 2,
        ),
        out_shape=[shape((hidden, NX * NZ * 96))] * 2,
        cost_estimate=cost(2 * 16 * 384 * 512 * 144, 4 * MIB),
        compiler_params=params(),
        name="split_down",
    )(where, mine, in_hbm(theirs), after)


def split_up_kernel(where_ref, mine_ref, theirs_ref, after_ref, out_ref, done_ref):
    done_ref[...] = jnp.zeros_like(done_ref)
    pick = own_blocks(where_ref[0])
    rows = mine_ref.shape[0]
    for part in range(2):
        for side, weight_ref in enumerate((mine_ref, theirs_ref)):
            weight = weight_ref[:, part * 768 : part * 768 + 768]
            out_ref[side * rows : (side + 1) * rows, part * 384 : part * 384 + 384] = jnp.dot(
                weight, pick, preferred_element_type=F32
            ).astype(BF16)


def split_up(where, mine, theirs, after):
    rows, width = mine.shape
    weights = pl.BlockSpec((rows, 1536), lambda i: (0, i))
    return pl.pallas_call(
        split_up_kernel,
        grid=(width // 1536,),
        in_specs=[smem_spec(), weights, weights, any_spec()],
        out_specs=[pl.BlockSpec((2 * rows, 768), lambda i: (0, i)), pl.BlockSpec((8, 128), lambda i: (0, 0))],
        out_shape=[shape((2 * rows, width // 2)), shape((8, 128), F32)],
        cost_estimate=cost(2 * 576 * 6144 * 768, 11 * MIB),
        compiler_params=params(16),
        name="split_up",
    )(where, in_hbm(mine), in_hbm(theirs), after)


def project_kernel(keep_ref, other_ref, mine_ref, theirs_ref, out_ref):
    blocks = keep_ref.shape[0]
    mine, theirs = mine_ref[:64], theirs_ref[:64]
    total = nt_dot(keep_ref[...].reshape(blocks * 96, 128), jnp.concatenate([mine, mine], 0))
    total += nt_dot(other_ref[...].reshape(blocks * 96, 128), jnp.concatenate([theirs, theirs], 0))
    total = total.reshape(blocks, 96, 128)
    left = lax.broadcasted_iota(jnp.int32, (blocks, 48, 128), 2) < 64
    total = jnp.where(left, total[:, :48], total[:, 48:]).astype(BF16)
    for column in range(blocks // NZ):
        out_ref[:, column] = total[column * NZ : (column + 1) * NZ]


def project(keep, other, mine, theirs):
    block = 16
    weights = pl.BlockSpec((block, 96, 128), lambda i: (i, 0, 0))
    tokens = pl.BlockSpec((192, 128), lambda i: (0, 0))
    return pl.pallas_call(
        project_kernel,
        grid=(NX * NZ // block,),
        in_specs=[weights, weights, tokens, tokens],
        out_specs=pl.BlockSpec((NZ, block // NZ, 48, 128), lambda i: (0, i, 0, 0)),
        out_shape=shape((NZ, NX, 48, 128)),
        cost_estimate=cost(2 * 3072 * 256 * 128, 2 * MIB),
        compiler_params=params(),
        name="project",
    )(keep, other, mine, theirs)


def project_rest_kernel(where_ref, keep_ref, other_ref, mine_ref, theirs_ref, after_ref, *out_refs):
    for far, out_ref in enumerate(out_refs):
        start = lax.rem(where_ref[1] + far, NX) * NZ
        total = nt_dot(keep_ref[pl.ds(start, NZ)].reshape(NZ * 96, 128), mine_ref[64:])
        total += nt_dot(other_ref[pl.ds(start, NZ)].reshape(NZ * 96, 128), theirs_ref[64:])
        out_ref[...] = total.astype(BF16).reshape(NZ, 96, 128)


def project_rest(where, keep, other, mine, theirs, after):
    return pl.pallas_call(
        project_rest_kernel,
        in_specs=[smem_spec()] + [vmem_spec()] * 4 + [any_spec()],
        out_specs=[vmem_spec()] * NX,
        out_shape=[shape((NZ, 96, 128))] * NX,
        cost_estimate=cost(2 * 3072 * 256 * 128, 3 * MIB),
        compiler_params=params(),
        name="project_rest",
    )(where, keep, other, mine, theirs, after)


def add_rest_kernel(*refs):
    in_refs, out_ref = refs[:-1], refs[-1]
    blank = jnp.zeros((32, 128), F32)
    for block in range(NZ):
        total = sum(in_ref[block].astype(F32) for in_ref in in_refs)
        total = jnp.concatenate([total, blank], 0).T
        out_ref[:, block] = total.astype(BF16).reshape(4, 32, 128)


def add_rest(parts):
    return pl.pallas_call(
        add_rest_kernel,
        in_specs=[vmem_spec()] * NX,
        out_specs=vmem_spec(),
        out_shape=shape((4, NZ, 32, 128)),
        cost_estimate=cost(MIB, MIB),
        compiler_params=params(),
        name="add_rest",
    )(*parts)


def residual_kernel(in_ref, hidden_ref, one_ref, two_ref, three_ref, send_ref):
    routed = (jnp.sum(in_ref[...].astype(F32), 0) + hidden_ref[...]).astype(BF16)
    for copy in range(send_ref.shape[0]):
        send_ref[copy] = routed


def routed_residual(parts, hidden, *after):
    return pl.pallas_call(
        residual_kernel,
        in_specs=[vmem_spec()] * 2 + [any_spec()] * 3,
        out_specs=vmem_spec(),
        out_shape=shape((NX * NZ, 48, 128)),
        cost_estimate=cost(MIB, MIB),
        compiler_params=params(),
        name="routed_residual",
    )(parts, hidden, *after)


def up_kernel(features_ref, weight_ref, after_ref, out_ref):
    rows, blocks = weight_ref.shape[0], features_ref.shape[0]
    step = blocks // 2
    left = lax.broadcasted_iota(jnp.int32, (48, 128), 1) < 64
    zero = jnp.zeros((48, 128), BF16)
    total = jnp.zeros((rows, 128), F32)
    square = jnp.zeros((8, 128), F32)
    for start in range(0, blocks, step):
        pieces = []
        for block in range(start, start + step):
            part = features_ref[block % NZ * NX + block // NZ]
            pieces += [jnp.where(left, part, zero), jnp.where(left, zero, part)]
            wide = part.astype(F32)
            square += jnp.sum((wide * wide).reshape(6, 8, 128), 0)
        weight = weight_ref[:, start * 96 : (start + step) * 96]
        total += jnp.dot(weight, jnp.concatenate(pieces, 0), preferred_element_type=F32)
    square = jnp.broadcast_to(jnp.sum(square, 0, keepdims=True), (8, 128))
    out_ref[:rows] = total[:, :64] + total[:, 64:]
    out_ref[rows:] = square[:, :64] + square[:, 64:]


def up_project(features, weight, after):
    rows = weight.shape[0]
    return pl.pallas_call(
        up_kernel,
        in_specs=[vmem_spec(), vmem_spec(), any_spec()],
        out_specs=vmem_spec(),
        out_shape=shape((rows + 8, 64), F32),
        cost_estimate=cost(2 * 576 * 3072 * 128, 5 * MIB),
        compiler_params=params(16),
        name="up_project",
    )(features, weight, after)


def down_kernel(mine_ref, theirs_ref, keep_ref, other_ref, *out_refs):
    rows = (mine_ref.shape[0] - 8) // 2
    square = mine_ref[2 * rows : 2 * rows + 1] + theirs_ref[2 * rows : 2 * rows + 1]
    scale = lax.rsqrt(square / 6144.0 + EPSILON_NORM)
    total = jnp.zeros((64, keep_ref.shape[1]), F32)
    for one, two, weight_ref in ((0, rows, keep_ref), (rows, 0, other_ref)):
        product = (mine_ref[one : one + rows] + theirs_ref[two : two + rows]) * scale
        hidden = (silu(product[: rows // 2]) * product[rows // 2 :]).astype(BF16)
        total += tn_dot(hidden, weight_ref[...])
    total = total.astype(BF16)
    width = NZ * 96
    for step in range(2):

        @pl.when(pl.program_id(0) == step)
        def _():
            for column in range(2):
                out_refs[2 * step + column][...] = total[:, column * width : (column + 1) * width]


def down_project(mine, theirs, keep, other):
    hidden, width = keep.shape
    products = pl.BlockSpec(mine.shape, lambda i: (0, 0))
    weights = pl.BlockSpec((hidden, width // 2), lambda i: (0, i))
    return pl.pallas_call(
        down_kernel,
        grid=(2,),
        in_specs=[products, products, weights, weights],
        out_specs=[pl.BlockSpec((64, NZ * 96), lambda i: (0, 0))] * NX,
        out_shape=[shape((64, NZ * 96))] * NX,
        cost_estimate=cost(2 * 288 * 3072 * 64, 3 * MIB),
        compiler_params=params(16),
        name="down_project",
    )(mine, theirs, keep, other)


def merge_kernel(rest_ref, *refs):
    in_refs, out_ref = refs[:-1], refs[-1]
    out_ref[:, :, :32] = rest_ref[...]
    row = lax.broadcasted_iota(jnp.int32, (384, 512), 0)
    lane = lax.broadcasted_iota(jnp.int32, (384, 512), 1)
    spread = one_hot((row == lane // 128 * 96 + lane % 128) & (lane % 128 < 96))
    for half in range(2):
        total = sum(in_ref[:, half * 384 : half * 384 + 384].astype(F32) for in_ref in in_refs).astype(BF16)
        total = jnp.dot(total, spread, preferred_element_type=F32).astype(BF16)
        for block in range(4):
            part = total[:, block * 128 : block * 128 + 128]
            out_ref[:, half * 4 + block, 32:] = part.reshape(4, 16, 128)


def merge(rest, parts):
    return pl.pallas_call(
        merge_kernel,
        in_specs=[vmem_spec()] * (1 + NX),
        out_specs=vmem_spec(),
        out_shape=shape((4, NZ, 48, 128)),
        cost_estimate=cost(MIB, MIB),
        compiler_params=params(),
        name="merge",
    )(rest, *parts)


def combine_kernel(parts_ref, place_ref, weight_ref, hidden_ref, out_ref):
    parts = jnp.sum(parts_ref[...].astype(F32), 1)
    residual = hidden_ref[...].astype(F32) + parts[:, :32].reshape(128, 128)
    result = parts[:, 32:].astype(BF16).reshape(64, 128)
    fetched = jnp.dot(place_ref[:, :64], result, preferred_element_type=F32)
    out_ref[...] = (residual + weight_ref[...] * fetched)[:, :96].astype(BF16)


def combine(parts, place, weight, hidden):
    return pl.pallas_call(
        combine_kernel,
        in_specs=[vmem_spec()] * 4,
        out_specs=vmem_spec(),
        out_shape=shape((128, 96)),
        cost_estimate=cost(MIB, MIB),
        compiler_params=params(),
        name="combine",
    )(parts, place, weight, hidden)


def gate_kernel(value_ref, after_ref, out_ref):
    out_ref[...] = value_ref[...]


def gate(value, after):
    return pl.pallas_call(
        gate_kernel,
        in_specs=[vmem_spec(), any_spec()],
        out_specs=vmem_spec(),
        out_shape=jax.ShapeDtypeStruct(value.shape, value.dtype),
        compiler_params=params(4),
        name="gate",
    )(value, after)


def swap(value):
    return lax.ppermute(value, "core", [(0, 1), (1, 0)])


def shifted(blocks, axis):
    count = len(blocks)
    return [blocks[0]] + [
        lax.ppermute(blocks[far], axis, [(i, (i + far) % count) for i in range(count)]) for far in range(1, count)
    ]


def per_device(
    unfinished, states, qkv_rows, decay_rate, out_weight, hidden_in, routes, route_weight, expert_up, expert_down
):
    where = jnp.stack([lax.axis_index(axis).astype(jnp.int32) for axis in ("core", "x", "dp")])

    with jax.named_scope("attention"):
        local = attend(states[0], qkv_rows[0].transpose(0, 2, 1, 3))
        parts = lax.all_to_all(local, HEAD, 0, 0, tiled=True)
    with jax.named_scope("weights"):
        keep_out, other_out = split_out(where, out_weight, swap(out_weight), local)
    with jax.named_scope("routing"):
        hidden = jnp.pad(hidden_in.transpose(1, 2, 0).reshape(128, 96), ((0, 0), (0, 32)))
        slots = jnp.repeat(unfinished, 4)[:, None]
        place, weight, facts = route(routes.reshape(128, 2), route_weight.reshape(128, 2), hidden, slots)
    with jax.named_scope("heads"):
        head_out = decay_heads(where, decay_rate, parts, facts, keep_out)
        head_rows = [rows.reshape(-1, 128) for rows in shifted(head_out, "dp")]
        mine, routed_hidden = select(where, head_rows)
        theirs = swap(mine)
    with jax.named_scope("projection"):
        partial = project(keep_out, other_out, mine, theirs)
        summed = lax.all_to_all(partial.reshape(NZ * NX, 48, 128), ("z", "x"), 0, 0, tiled=True)
        keep_down, other_down = split_down(where, expert_down[0], swap(expert_down[0]), partial)
        rest = project_rest(where, keep_out, other_out, mine, theirs, partial)
        rest = shifted(rest, "x")
        routed = routed_residual(summed, routed_hidden, rest[1], rest[3], keep_down)
    with jax.named_scope("expert"):
        up = expert_up[0].transpose(1, 2, 0).reshape(288, 6144)
        up, split = split_up(where, up, swap(up), routed)
        features = gate(lax.all_to_all(routed, ("z", "x"), 0, 0, tiled=True), rest[2])
        products = up_project(features, up, swap(split))
        results = down_project(products, swap(products), keep_down, other_down)
        rest = add_rest(rest)
        merged = merge(rest, shifted(results, "x")).reshape(32, 48, 128)
        returned = lax.all_to_all(merged, ("dp", "z"), 0, 0, tiled=True)
    with jax.named_scope("output"):
        mixed = combine(returned.reshape(4, NZ, 48, 128), place, weight, hidden)
        return mixed.reshape(32, 4, 96).transpose(2, 0, 1)


def solution(mesh):
    grid = Mesh(mesh.devices.reshape(mesh.shape["dp"], NX, NZ, NC), EVERY)
    return jax.shard_map(
        per_device,
        mesh=grid,
        in_specs=(
            P("dp"),
            P(EVERY, None, None, None),
            P(EVERY, None, None, None, None),
            P(HEAD),
            P(HEAD, None),
            P(HEAD, "dp", None),
            P("dp", None, None),
            P("dp", None, None),
            P("dp", None, None, HEAD),
            P("dp", HEAD, None),
        ),
        out_specs=P(HEAD, "dp", None),
        check_vma=False,
    )
```

```python
import functools

import jax
import jax.numpy as jnp
from jax import lax
from jax.experimental import pallas as pl
from jax.experimental.pallas import tpu as pltpu
from jax.sharding import Mesh, PartitionSpec as P

EPSILON_HEAD = 1e-06
EPSILON_NORM = 1e-05
BF16, F32 = jnp.bfloat16, jnp.float32
NX, NZ, NC = 4, 8, 2
EVERY = ("dp", "x", "z", "core")
HEAD = ("x", "z", "core")
MIB = 1 << 20


def vmem_spec():
    return pl.BlockSpec(memory_space=pltpu.VMEM)


def smem_spec():
    return pl.BlockSpec(memory_space=pltpu.SMEM)


def any_spec():
    return pl.BlockSpec(memory_space=pl.ANY)


def in_hbm(value):
    return pltpu.with_memory_space_constraint(value, pltpu.HBM)


def params(mib=12):
    return pltpu.CompilerParams(vmem_limit_bytes=mib * MIB)


def cost(flops, size):
    return pl.CostEstimate(flops=flops, bytes_accessed=size, transcendentals=0)


def shape(dims, dtype=BF16):
    return jax.ShapeDtypeStruct(dims, dtype)


def nt_dot(left, right):
    return lax.dot_general(left, right, (((1,), (1,)), ((), ())), preferred_element_type=F32)


def tn_dot(left, right):
    return lax.dot_general(left, right, (((0,), (0,)), ((), ())), preferred_element_type=F32)


def silu(value):
    return value / (1.0 + jnp.exp(-value))


def one_hot(mask):
    return mask.astype(F32).astype(BF16)


def attend_kernel(state_ref, input_ref, out_ref):
    heads = state_ref.shape[0]
    query = silu(input_ref[:, 0].astype(F32))
    key = silu(input_ref[:, 1].astype(F32))
    high = query.astype(BF16).astype(F32)
    both = jnp.concatenate([high, query - high], 1).astype(BF16)
    for head in range(heads):
        base = jnp.dot(both[head], state_ref[head], preferred_element_type=F32)
        out_ref[head, 0] = (base[:4] + base[4:]).astype(BF16)
    out_ref[:, 1] = input_ref[:, 2]
    lane = lax.broadcasted_iota(jnp.int32, query.shape, 2)
    cross = jnp.zeros(query.shape, F32)
    for source in range(4):
        weight = jnp.sum(query * key[:, source : source + 1], -1, keepdims=True)
        whole = weight.astype(BF16).astype(F32)
        cross = jnp.where(lane == source, whole, cross)
        cross = jnp.where(lane == source + 4, weight - whole, cross)
    out_ref[:, 2] = cross.astype(BF16)


def attend(states, inputs):
    heads, block = states.shape[0], 32
    return pl.pallas_call(
        attend_kernel,
        grid=(heads // block,),
        in_specs=[
            pl.BlockSpec((block, 128, 128), lambda i: (i, 0, 0)),
            pl.BlockSpec((block, 3, 4, 128), lambda i: (i, 0, 0, 0)),
        ],
        out_specs=pl.BlockSpec((block, 3, 4, 128), lambda i: (i, 0, 0, 0)),
        out_shape=shape((heads, 3, 4, 128)),
        cost_estimate=cost(2 * 8 * 64 * 128 * 128, 3 * MIB),
        compiler_params=params(),
        name="attend",
    )(in_hbm(states), in_hbm(inputs))


def decay_kernel(where_ref, rate_ref, parts_ref, facts_ref, after_ref, *out_refs):
    slots = parts_ref.shape[0]
    rate = jnp.full((4, 128), rate_ref[0], F32)
    step = lax.broadcasted_iota(jnp.int32, (4, 128), 0).astype(F32)
    value = parts_ref[:, 1].astype(F32)
    cross = parts_ref[:, 2].astype(F32)
    cross += pltpu.roll(cross, 124, 2)
    attn = jnp.exp(-rate * (step + 1.0)) * parts_ref[:, 0].astype(F32)
    for source in range(4):
        factor = jnp.where(step >= source, jnp.exp(-rate * jnp.maximum(step - source, 0.0)), 0.0)
        attn += (factor * cross[:, :, source : source + 1]) * value[:, source : source + 1]
    scaled = attn * lax.rsqrt(jnp.mean(attn * attn, -1, keepdims=True) + EPSILON_HEAD)
    scaled = scaled.astype(BF16)
    for far, out_ref in enumerate(out_refs):
        out_ref[:slots] = scaled
        out_ref[slots:] = facts_ref[lax.rem(where_ref[2] + far, 4)]


def decay_heads(where, rate, parts, facts, after):
    slots = parts.shape[0]
    return pl.pallas_call(
        decay_kernel,
        in_specs=[smem_spec(), smem_spec(), vmem_spec(), vmem_spec(), any_spec()],
        out_specs=[vmem_spec()] * 4,
        out_shape=[shape((slots + 4, 4, 128))] * 4,
        cost_estimate=cost(4 * MIB, MIB),
        compiler_params=params(),
        name="decay_heads",
    )(where, rate, parts, facts, after)


def route_kernel(pair_ref, weight_ref, hidden_ref, row_ref, place_ref, factor_ref, out_ref):
    pair = pair_ref[...]
    expert = jnp.min(pair, 1, keepdims=True)
    factor_ref[...] = jnp.sum(jnp.where(pair < 4, weight_ref[...], 0.0), 1, keepdims=True)
    token = lax.broadcasted_iota(jnp.int32, (128, 128), 0)
    lane = lax.broadcasted_iota(jnp.int32, (128, 128), 1)
    named = (lane == expert).astype(F32)
    ranks = jnp.dot(one_hot(token > lane), named.astype(BF16), preferred_element_type=F32)
    rank = jnp.sum(ranks * named, 1, keepdims=True).astype(jnp.int32)
    position = jnp.where(expert < 4, expert * 16 + rank, -1)
    place = one_hot(lane == position)
    place_ref[...] = place
    row = row_ref[...].astype(F32)
    facts = hidden_ref[...].astype(F32)
    facts = jnp.where(lane == 96, row, jnp.where(lane == 97, (token % 4).astype(F32), facts))
    slots = jnp.where(lane == 98, row, 0.0)
    quarter = one_hot((token % 16 < 8) & (lane == (token // 16 * 8 + token % 16) * 4))
    packed = tn_dot(place, facts.astype(BF16)) + jnp.dot(quarter, slots.astype(BF16), preferred_element_type=F32)
    out_ref[...] = packed[:64].reshape(4, 4, 4, 128).astype(BF16)


def route(pair, weight, hidden, row):
    return pl.pallas_call(
        route_kernel,
        in_specs=[vmem_spec()] * 4,
        out_specs=[vmem_spec()] * 3,
        out_shape=[shape((128, 128)), shape((128, 1), F32), shape((4, 4, 4, 128))],
        cost_estimate=cost(8 * MIB, MIB // 2),
        compiler_params=params(),
        name="route",
    )(pair, weight, hidden, row)


def select_kernel(where_ref, *refs):
    in_refs, (out_ref, hidden_ref, held_ref) = refs[:4], refs[4:]
    span = held_ref.shape[1]
    steps = span - 16
    for far, in_ref in enumerate(in_refs):
        held_ref[lax.rem(where_ref[2] + (4 - far), 4)] = in_ref[...]
    rows = held_ref[...].reshape(4 * span, 128)
    facts = held_ref[:, steps:].reshape(64, 128)
    held = facts.astype(F32)
    token = lax.broadcasted_iota(jnp.int32, (128, 64), 0)
    source = lax.broadcasted_iota(jnp.int32, (128, 64), 1)
    spread = one_hot(source == token // 32 * 16 + token % 32 // 4)
    rest = jnp.dot(spread, facts, preferred_element_type=F32)
    step = (lax.broadcasted_iota(jnp.int32, (128, 1), 0) % 4).astype(F32)
    row = jnp.concatenate([held[:, 96:97], rest[:, 98:99]], 0)
    step = jnp.concatenate([held[:, 97:98], step], 0)
    row = (row * 4.0 + step).astype(jnp.int32)
    row = row // steps * span + row % steps
    lane = lax.broadcasted_iota(jnp.int32, (192, 4 * span), 1)
    out_ref[...] = jnp.dot(one_hot(lane == row), rows, preferred_element_type=F32).astype(BF16)
    turned = jnp.concatenate([held, held], 0).T
    left = lax.broadcasted_iota(jnp.int32, (48, 128), 1) < 64
    hidden_ref[...] = jnp.where(left, turned[:48], turned[48:96])


def select(where, parts):
    return pl.pallas_call(
        select_kernel,
        in_specs=[smem_spec()] + [vmem_spec()] * 4,
        out_specs=[vmem_spec()] * 2,
        out_shape=[shape((192, 128)), shape((48, 128), F32)],
        scratch_shapes=[pltpu.VMEM((4,) + parts[0].shape, BF16)],
        cost_estimate=cost(2 * 192 * 1088 * 128, MIB),
        compiler_params=params(),
        name="select",
    )(where, *parts)


def split_out_kernel(where_ref, mine_ref, theirs_ref, after_ref, *out_refs):
    core = where_ref[0]
    row = lax.broadcasted_iota(jnp.int32, (192, 384), 0)
    lane = lax.broadcasted_iota(jnp.int32, (192, 384), 1)
    pick = one_hot(lane == row // 96 * 192 + row % 96 + core * 96)
    for part in range(8):
        for weight_ref, out_ref in zip((mine_ref, theirs_ref), out_refs):
            weight = weight_ref[:, part * 384 : part * 384 + 384]
            out_ref[2 * part : 2 * part + 2] = nt_dot(pick, weight).astype(BF16).reshape(2, 96, 128)


def split_out(where, mine, theirs, after):
    return pl.pallas_call(
        split_out_kernel,
        grid=(2,),
        in_specs=[smem_spec()] + [pl.BlockSpec((128, 3072), lambda i: (0, i))] * 2 + [any_spec()],
        out_specs=[pl.BlockSpec((16, 96, 128), lambda i: (i, 0, 0))] * 2,
        out_shape=[shape((NX * NZ, 96, 128))] * 2,
        cost_estimate=cost(2 * 16 * 384 * 384 * 128, 3 * MIB),
        compiler_params=params(),
        name="split_out",
    )(where, mine, in_hbm(theirs), after)


def own_blocks(core):
    row = lax.broadcasted_iota(jnp.int32, (768, 384), 0)
    lane = lax.broadcasted_iota(jnp.int32, (768, 384), 1)
    return one_hot(row == lane // 96 * 192 + lane % 96 + core * 96)


def split_down_kernel(where_ref, mine_ref, theirs_ref, after_ref, *out_refs):
    pick = own_blocks(where_ref[0])
    for part in range(2):
        for weight_ref, out_ref in zip((mine_ref, theirs_ref), out_refs):
            weight = weight_ref[:, part * 768 : part * 768 + 768]
            out_ref[:, part * 384 : part * 384 + 384] = jnp.dot(weight, pick, preferred_element_type=F32).astype(BF16)


def split_down(where, mine, theirs, after):
    hidden = mine.shape[0]
    weights = pl.BlockSpec((hidden, 1536), lambda i, where: (0, lax.rem(where[1] + i, NX)))
    return pl.pallas_call(
        split_down_kernel,
        grid_spec=pltpu.PrefetchScalarGridSpec(
            num_scalar_prefetch=1,
            grid=(NX,),
            in_specs=[weights, weights, any_spec()],
            out_specs=[pl.BlockSpec((hidden, NZ * 96), lambda i, where: (0, i))] * 2,
        ),
        out_shape=[shape((hidden, NX * NZ * 96))] * 2,
        cost_estimate=cost(2 * 16 * 384 * 512 * 144, 4 * MIB),
        compiler_params=params(),
        name="split_down",
    )(where, mine, in_hbm(theirs), after)


def split_up_kernel(where_ref, mine_ref, theirs_ref, after_ref, out_ref, done_ref):
    done_ref[...] = jnp.zeros_like(done_ref)
    pick = own_blocks(where_ref[0])
    rows = mine_ref.shape[0]
    for part in range(2):
        for side, weight_ref in enumerate((mine_ref, theirs_ref)):
            weight = weight_ref[:, part * 768 : part * 768 + 768]
            out_ref[side * rows : (side + 1) * rows, part * 384 : part * 384 + 384] = jnp.dot(
                weight, pick, preferred_element_type=F32
            ).astype(BF16)


def split_up(where, mine, theirs, after):
    rows, width = mine.shape
    weights = pl.BlockSpec((rows, 1536), lambda i: (0, i))
    return pl.pallas_call(
        split_up_kernel,
        grid=(width // 1536,),
        in_specs=[smem_spec(), weights, weights, any_spec()],
        out_specs=[pl.BlockSpec((2 * rows, 768), lambda i: (0, i)), pl.BlockSpec((8, 128), lambda i: (0, 0))],
        out_shape=[shape((2 * rows, width // 2)), shape((8, 128), F32)],
        cost_estimate=cost(2 * 576 * 6144 * 768, 11 * MIB),
        compiler_params=params(16),
        name="split_up",
    )(where, in_hbm(mine), in_hbm(theirs), after)


def project_kernel(keep_ref, other_ref, mine_ref, theirs_ref, out_ref):
    blocks = keep_ref.shape[0]
    mine, theirs = mine_ref[:64], theirs_ref[:64]
    total = nt_dot(keep_ref[...].reshape(blocks * 96, 128), jnp.concatenate([mine, mine], 0))
    total += nt_dot(other_ref[...].reshape(blocks * 96, 128), jnp.concatenate([theirs, theirs], 0))
    total = total.reshape(blocks, 96, 128)
    left = lax.broadcasted_iota(jnp.int32, (blocks, 48, 128), 2) < 64
    total = jnp.where(left, total[:, :48], total[:, 48:]).astype(BF16)
    for column in range(blocks // NZ):
        out_ref[:, column] = total[column * NZ : (column + 1) * NZ]


def project(keep, other, mine, theirs):
    block = 16
    weights = pl.BlockSpec((block, 96, 128), lambda i: (i, 0, 0))
    tokens = pl.BlockSpec((192, 128), lambda i: (0, 0))
    return pl.pallas_call(
        project_kernel,
        grid=(NX * NZ // block,),
        in_specs=[weights, weights, tokens, tokens],
        out_specs=pl.BlockSpec((NZ, block // NZ, 48, 128), lambda i: (0, i, 0, 0)),
        out_shape=shape((NZ, NX, 48, 128)),
        cost_estimate=cost(2 * 3072 * 256 * 128, 2 * MIB),
        compiler_params=params(),
        name="project",
    )(keep, other, mine, theirs)


def project_rest_kernel(where_ref, keep_ref, other_ref, mine_ref, theirs_ref, after_ref, *out_refs):
    for far, out_ref in enumerate(out_refs):
        start = lax.rem(where_ref[1] + far, NX) * NZ
        total = nt_dot(keep_ref[pl.ds(start, NZ)].reshape(NZ * 96, 128), mine_ref[64:])
        total += nt_dot(other_ref[pl.ds(start, NZ)].reshape(NZ * 96, 128), theirs_ref[64:])
        out_ref[...] = total.astype(BF16).reshape(NZ, 96, 128)


def project_rest(where, keep, other, mine, theirs, after):
    return pl.pallas_call(
        project_rest_kernel,
        in_specs=[smem_spec()] + [vmem_spec()] * 4 + [any_spec()],
        out_specs=[vmem_spec()] * NX,
        out_shape=[shape((NZ, 96, 128))] * NX,
        cost_estimate=cost(2 * 3072 * 256 * 128, 3 * MIB),
        compiler_params=params(),
        name="project_rest",
    )(where, keep, other, mine, theirs, after)


def add_rest_kernel(*refs):
    in_refs, out_ref = refs[:-1], refs[-1]
    blank = jnp.zeros((32, 128), F32)
    for block in range(NZ):
        total = sum(in_ref[block].astype(F32) for in_ref in in_refs)
        total = jnp.concatenate([total, blank], 0).T
        out_ref[:, block] = total.astype(BF16).reshape(4, 32, 128)


def add_rest(parts):
    return pl.pallas_call(
        add_rest_kernel,
        in_specs=[vmem_spec()] * NX,
        out_specs=vmem_spec(),
        out_shape=shape((4, NZ, 32, 128)),
        cost_estimate=cost(MIB, MIB),
        compiler_params=params(),
        name="add_rest",
    )(*parts)


def residual_kernel(in_ref, hidden_ref, one_ref, two_ref, three_ref, send_ref, held_ref, sems):
    routed = (jnp.sum(in_ref[...].astype(F32), 0) + hidden_ref[...]).astype(BF16)
    span = held_ref.shape[0]
    for copy in range(span):
        held_ref[copy] = routed
    copies = [
        pltpu.make_async_copy(held_ref, send_ref.at[pl.ds(index * span, span)], sems.at[index])
        for index in range(NX * NZ // span)
    ]
    for copy in copies:
        copy.start()
    for copy in copies:
        copy.wait()


def routed_residual(parts, hidden, *after):
    return pl.pallas_call(
        residual_kernel,
        in_specs=[vmem_spec()] * 2 + [any_spec()] * 3,
        out_specs=any_spec(),
        out_shape=shape((NX * NZ, 48, 128)),
        scratch_shapes=[pltpu.VMEM((4, 48, 128), BF16), pltpu.SemaphoreType.DMA((8,))],
        cost_estimate=cost(MIB, MIB),
        compiler_params=params(),
        name="routed_residual",
    )(parts, hidden, *after)


def up_kernel(features_ref, weight_ref, after_ref, out_ref):
    rows, blocks = weight_ref.shape[0], features_ref.shape[0]
    step = blocks // 2
    left = lax.broadcasted_iota(jnp.int32, (48, 128), 1) < 64
    zero = jnp.zeros((48, 128), BF16)
    total = jnp.zeros((rows, 128), F32)
    square = jnp.zeros((8, 128), F32)
    for start in range(0, blocks, step):
        pieces = []
        for block in range(start, start + step):
            part = features_ref[block % NZ * NX + block // NZ]
            pieces += [jnp.where(left, part, zero), jnp.where(left, zero, part)]
            wide = part.astype(F32)
            square += jnp.sum((wide * wide).reshape(6, 8, 128), 0)
        weight = weight_ref[:, start * 96 : (start + step) * 96]
        total += jnp.dot(weight, jnp.concatenate(pieces, 0), preferred_element_type=F32)
    square = jnp.broadcast_to(jnp.sum(square, 0, keepdims=True), (8, 128))
    out_ref[:rows] = total[:, :64] + total[:, 64:]
    out_ref[rows:] = square[:, :64] + square[:, 64:]


def up_project(features, weight, after):
    rows = weight.shape[0]
    return pl.pallas_call(
        up_kernel,
        in_specs=[vmem_spec(), vmem_spec(), any_spec()],
        out_specs=vmem_spec(),
        out_shape=shape((rows + 8, 64), F32),
        cost_estimate=cost(2 * 576 * 3072 * 128, 5 * MIB),
        compiler_params=params(16),
        name="up_project",
    )(features, weight, after)


def down_kernel(mine_ref, theirs_ref, keep_ref, other_ref, *out_refs):
    rows = (mine_ref.shape[0] - 8) // 2
    square = mine_ref[2 * rows : 2 * rows + 1] + theirs_ref[2 * rows : 2 * rows + 1]
    scale = lax.rsqrt(square / 6144.0 + EPSILON_NORM)
    total = jnp.zeros((64, keep_ref.shape[1]), F32)
    for one, two, weight_ref in ((0, rows, keep_ref), (rows, 0, other_ref)):
        product = (mine_ref[one : one + rows] + theirs_ref[two : two + rows]) * scale
        hidden = (silu(product[: rows // 2]) * product[rows // 2 :]).astype(BF16)
        total += tn_dot(hidden, weight_ref[...])
    total = total.astype(BF16)
    width = NZ * 96
    for step in range(2):

        @pl.when(pl.program_id(0) == step)
        def _():
            for column in range(2):
                out_refs[2 * step + column][...] = total[:, column * width : (column + 1) * width]


def down_project(mine, theirs, keep, other):
    hidden, width = keep.shape
    products = pl.BlockSpec(mine.shape, lambda i: (0, 0))
    weights = pl.BlockSpec((hidden, width // 2), lambda i: (0, i))
    return pl.pallas_call(
        down_kernel,
        grid=(2,),
        in_specs=[products, products, weights, weights],
        out_specs=[pl.BlockSpec((64, NZ * 96), lambda i: (0, 0))] * NX,
        out_shape=[shape((64, NZ * 96))] * NX,
        cost_estimate=cost(2 * 288 * 3072 * 64, 3 * MIB),
        compiler_params=params(16),
        name="down_project",
    )(mine, theirs, keep, other)


def merge_kernel(rest_ref, *refs):
    in_refs, out_ref = refs[:-1], refs[-1]
    out_ref[:, :, :32] = rest_ref[...]
    row = lax.broadcasted_iota(jnp.int32, (384, 512), 0)
    lane = lax.broadcasted_iota(jnp.int32, (384, 512), 1)
    spread = one_hot((row == lane // 128 * 96 + lane % 128) & (lane % 128 < 96))
    for half in range(2):
        total = sum(in_ref[:, half * 384 : half * 384 + 384].astype(F32) for in_ref in in_refs).astype(BF16)
        total = jnp.dot(total, spread, preferred_element_type=F32).astype(BF16)
        for block in range(4):
            part = total[:, block * 128 : block * 128 + 128]
            out_ref[:, half * 4 + block, 32:] = part.reshape(4, 16, 128)


def merge(rest, parts):
    return pl.pallas_call(
        merge_kernel,
        in_specs=[vmem_spec()] * (1 + NX),
        out_specs=vmem_spec(),
        out_shape=shape((4, NZ, 48, 128)),
        cost_estimate=cost(MIB, MIB),
        compiler_params=params(),
        name="merge",
    )(rest, *parts)


def combine_kernel(parts_ref, place_ref, weight_ref, hidden_ref, out_ref):
    parts = jnp.sum(parts_ref[...].astype(F32), 1)
    residual = hidden_ref[...].astype(F32) + parts[:, :32].reshape(128, 128)
    result = parts[:, 32:].astype(BF16).reshape(64, 128)
    fetched = jnp.dot(place_ref[:, :64], result, preferred_element_type=F32)
    out_ref[...] = (residual + weight_ref[...] * fetched)[:, :96].astype(BF16)


def combine(parts, place, weight, hidden):
    return pl.pallas_call(
        combine_kernel,
        in_specs=[vmem_spec()] * 4,
        out_specs=vmem_spec(),
        out_shape=shape((128, 96)),
        cost_estimate=cost(MIB, MIB),
        compiler_params=params(),
        name="combine",
    )(parts, place, weight, hidden)


def gate_kernel(value_ref, after_ref, out_ref):
    out_ref[...] = value_ref[...]


def gate(value, after):
    return pl.pallas_call(
        gate_kernel,
        in_specs=[vmem_spec(), any_spec()],
        out_specs=vmem_spec(),
        out_shape=jax.ShapeDtypeStruct(value.shape, value.dtype),
        compiler_params=params(4),
        name="gate",
    )(value, after)


def swap(value):
    return lax.ppermute(value, "core", [(0, 1), (1, 0)])


def shifted(blocks, axis):
    count = len(blocks)
    return [blocks[0]] + [
        lax.ppermute(blocks[far], axis, [(i, (i + far) % count) for i in range(count)]) for far in range(1, count)
    ]


def per_device(
    unfinished, states, qkv_rows, decay_rate, out_weight, hidden_in, routes, route_weight, expert_up, expert_down
):
    where = jnp.stack([lax.axis_index(axis).astype(jnp.int32) for axis in ("core", "x", "dp")])

    with jax.named_scope("attention"):
        local = attend(states[0], qkv_rows[0].transpose(0, 2, 1, 3))
        parts = lax.all_to_all(local, HEAD, 0, 0, tiled=True)
    with jax.named_scope("weights"):
        keep_out, other_out = split_out(where, out_weight, swap(out_weight), local)
    with jax.named_scope("routing"):
        hidden = jnp.pad(hidden_in.transpose(1, 2, 0).reshape(128, 96), ((0, 0), (0, 32)))
        slots = jnp.repeat(unfinished, 4)[:, None]
        place, weight, facts = route(routes.reshape(128, 2), route_weight.reshape(128, 2), hidden, slots)
    with jax.named_scope("heads"):
        head_out = decay_heads(where, decay_rate, parts, facts, keep_out)
        head_rows = [rows.reshape(-1, 128) for rows in shifted(head_out, "dp")]
        mine, routed_hidden = select(where, head_rows)
        theirs = swap(mine)
    with jax.named_scope("projection"):
        partial = project(keep_out, other_out, mine, theirs)
        summed = lax.all_to_all(partial.reshape(NZ * NX, 48, 128), ("z", "x"), 0, 0, tiled=True)
        keep_down, other_down = split_down(where, expert_down[0], swap(expert_down[0]), partial)
        rest = project_rest(where, keep_out, other_out, mine, theirs, partial)
        rest = shifted(rest, "x")
        routed = routed_residual(summed, routed_hidden, rest[1], rest[3], keep_down)
    with jax.named_scope("expert"):
        up = expert_up[0].transpose(1, 2, 0).reshape(288, 6144)
        up, split = split_up(where, up, swap(up), routed)
        features = gate(lax.all_to_all(routed, ("z", "x"), 0, 0, tiled=True), rest[2])
        products = up_project(features, up, swap(split))
        results = down_project(products, swap(products), keep_down, other_down)
        rest = add_rest(rest)
        merged = merge(rest, shifted(results, "x")).reshape(32, 48, 128)
        returned = lax.all_to_all(merged, ("dp", "z"), 0, 0, tiled=True)
    with jax.named_scope("output"):
        mixed = combine(returned.reshape(4, NZ, 48, 128), place, weight, hidden)
        return mixed.reshape(32, 4, 96).transpose(2, 0, 1)


def solution(mesh):
    grid = Mesh(mesh.devices.reshape(mesh.shape["dp"], NX, NZ, NC), EVERY)
    return jax.shard_map(
        per_device,
        mesh=grid,
        in_specs=(
            P("dp"),
            P(EVERY, None, None, None),
            P(EVERY, None, None, None, None),
            P(HEAD),
            P(HEAD, None),
            P(HEAD, "dp", None),
            P("dp", None, None),
            P("dp", None, None),
            P("dp", None, None, HEAD),
            P("dp", HEAD, None),
        ),
        out_specs=P(HEAD, "dp", None),
        check_vma=False,
    )
```

```python
import functools

import jax
import jax.numpy as jnp
from jax import lax
from jax.experimental import pallas as pl
from jax.experimental.pallas import tpu as pltpu
from jax.sharding import Mesh, PartitionSpec as P

EPSILON_HEAD = 1e-06
EPSILON_NORM = 1e-05
BF16, F32 = jnp.bfloat16, jnp.float32
NX, NZ, NC = 4, 8, 2
EVERY = ("dp", "x", "z", "core")
HEAD = ("x", "z", "core")
MIB = 1 << 20


def vmem_spec():
    return pl.BlockSpec(memory_space=pltpu.VMEM)


def smem_spec():
    return pl.BlockSpec(memory_space=pltpu.SMEM)


def any_spec():
    return pl.BlockSpec(memory_space=pl.ANY)


def in_hbm(value):
    return pltpu.with_memory_space_constraint(value, pltpu.HBM)


def params(mib=12):
    return pltpu.CompilerParams(vmem_limit_bytes=mib * MIB)


def cost(flops, size):
    return pl.CostEstimate(flops=flops, bytes_accessed=size, transcendentals=0)


def shape(dims, dtype=BF16):
    return jax.ShapeDtypeStruct(dims, dtype)


def nt_dot(left, right):
    return lax.dot_general(left, right, (((1,), (1,)), ((), ())), preferred_element_type=F32)


def tn_dot(left, right):
    return lax.dot_general(left, right, (((0,), (0,)), ((), ())), preferred_element_type=F32)


def silu(value):
    return value / (1.0 + jnp.exp(-value))


def one_hot(mask):
    return mask.astype(F32).astype(BF16)


def attend_kernel(state_ref, input_ref, out_ref):
    heads = state_ref.shape[0]
    query = silu(input_ref[:, 0].astype(F32))
    key = silu(input_ref[:, 1].astype(F32))
    high = query.astype(BF16).astype(F32)
    both = jnp.concatenate([high, query - high], 1).astype(BF16)
    for head in range(heads):
        base = jnp.dot(both[head], state_ref[head], preferred_element_type=F32)
        out_ref[head, 0] = (base[:4] + base[4:]).astype(BF16)
    out_ref[:, 1] = input_ref[:, 2]
    lane = lax.broadcasted_iota(jnp.int32, query.shape, 2)
    cross = jnp.zeros(query.shape, F32)
    for source in range(4):
        weight = jnp.sum(query * key[:, source : source + 1], -1, keepdims=True)
        whole = weight.astype(BF16).astype(F32)
        cross = jnp.where(lane == source, whole, cross)
        cross = jnp.where(lane == source + 4, weight - whole, cross)
    out_ref[:, 2] = cross.astype(BF16)


def attend(states, inputs):
    heads, block = states.shape[0], 32
    return pl.pallas_call(
        attend_kernel,
        grid=(heads // block,),
        in_specs=[
            pl.BlockSpec((block, 128, 128), lambda i: (i, 0, 0)),
            pl.BlockSpec((block, 3, 4, 128), lambda i: (i, 0, 0, 0)),
        ],
        out_specs=pl.BlockSpec((block, 3, 4, 128), lambda i: (i, 0, 0, 0)),
        out_shape=shape((heads, 3, 4, 128)),
        cost_estimate=cost(2 * 8 * 64 * 128 * 128, 3 * MIB),
        compiler_params=params(),
        name="attend",
    )(in_hbm(states), in_hbm(inputs))


def decay_kernel(where_ref, rate_ref, parts_ref, facts_ref, after_ref, *out_refs):
    slots = parts_ref.shape[0]
    rate = jnp.full((4, 128), rate_ref[0], F32)
    step = lax.broadcasted_iota(jnp.int32, (4, 128), 0).astype(F32)
    value = parts_ref[:, 1].astype(F32)
    cross = parts_ref[:, 2].astype(F32)
    cross += pltpu.roll(cross, 124, 2)
    attn = jnp.exp(-rate * (step + 1.0)) * parts_ref[:, 0].astype(F32)
    for source in range(4):
        factor = jnp.where(step >= source, jnp.exp(-rate * jnp.maximum(step - source, 0.0)), 0.0)
        attn += (factor * cross[:, :, source : source + 1]) * value[:, source : source + 1]
    scaled = attn * lax.rsqrt(jnp.mean(attn * attn, -1, keepdims=True) + EPSILON_HEAD)
    scaled = scaled.astype(BF16)
    for far, out_ref in enumerate(out_refs):
        out_ref[:slots] = scaled
        out_ref[slots:] = facts_ref[lax.rem(where_ref[2] + far, 4)]


def decay_heads(where, rate, parts, facts, after):
    slots = parts.shape[0]
    return pl.pallas_call(
        decay_kernel,
        in_specs=[smem_spec(), smem_spec(), vmem_spec(), vmem_spec(), any_spec()],
        out_specs=[vmem_spec()] * 4,
        out_shape=[shape((slots + 4, 4, 128))] * 4,
        cost_estimate=cost(4 * MIB, MIB),
        compiler_params=params(),
        name="decay_heads",
    )(where, rate, parts, facts, after)


def route_kernel(pair_ref, weight_ref, hidden_ref, row_ref, place_ref, factor_ref, out_ref):
    pair = pair_ref[...]
    expert = jnp.min(pair, 1, keepdims=True)
    factor_ref[...] = jnp.sum(jnp.where(pair < 4, weight_ref[...], 0.0), 1, keepdims=True)
    token = lax.broadcasted_iota(jnp.int32, (128, 128), 0)
    lane = lax.broadcasted_iota(jnp.int32, (128, 128), 1)
    named = (lane == expert).astype(F32)
    ranks = jnp.dot(one_hot(token > lane), named.astype(BF16), preferred_element_type=F32)
    rank = jnp.sum(ranks * named, 1, keepdims=True).astype(jnp.int32)
    position = jnp.where(expert < 4, expert * 16 + rank, -1)
    place = one_hot(lane == position)
    place_ref[...] = place
    row = row_ref[...].astype(F32)
    facts = hidden_ref[...].astype(F32)
    facts = jnp.where(lane == 96, row, jnp.where(lane == 97, (token % 4).astype(F32), facts))
    slots = jnp.where(lane == 98, row, 0.0)
    quarter = one_hot((token % 16 < 8) & (lane == (token // 16 * 8 + token % 16) * 4))
    packed = tn_dot(place, facts.astype(BF16)) + jnp.dot(quarter, slots.astype(BF16), preferred_element_type=F32)
    out_ref[...] = packed[:64].reshape(4, 4, 4, 128).astype(BF16)


def route(pair, weight, hidden, row):
    return pl.pallas_call(
        route_kernel,
        in_specs=[vmem_spec()] * 4,
        out_specs=[vmem_spec()] * 3,
        out_shape=[shape((128, 128)), shape((128, 1), F32), shape((4, 4, 4, 128))],
        cost_estimate=cost(8 * MIB, MIB // 2),
        compiler_params=params(),
        name="route",
    )(pair, weight, hidden, row)


def select_kernel(where_ref, *refs):
    in_refs, (out_ref, hidden_ref, held_ref) = refs[:4], refs[4:]
    span = held_ref.shape[1]
    steps = span - 16
    for far, in_ref in enumerate(in_refs):
        held_ref[lax.rem(where_ref[2] + (4 - far), 4)] = in_ref[...]
    rows = held_ref[...].reshape(4 * span, 128)
    facts = held_ref[:, steps:].reshape(64, 128)
    held = facts.astype(F32)
    token = lax.broadcasted_iota(jnp.int32, (128, 64), 0)
    source = lax.broadcasted_iota(jnp.int32, (128, 64), 1)
    spread = one_hot(source == token // 32 * 16 + token % 32 // 4)
    rest = jnp.dot(spread, facts, preferred_element_type=F32)
    step = (lax.broadcasted_iota(jnp.int32, (128, 1), 0) % 4).astype(F32)
    row = jnp.concatenate([held[:, 96:97], rest[:, 98:99]], 0)
    step = jnp.concatenate([held[:, 97:98], step], 0)
    row = (row * 4.0 + step).astype(jnp.int32)
    row = row // steps * span + row % steps
    lane = lax.broadcasted_iota(jnp.int32, (192, 4 * span), 1)
    out_ref[...] = jnp.dot(one_hot(lane == row), rows, preferred_element_type=F32).astype(BF16)
    turned = jnp.concatenate([held, held], 0).T
    left = lax.broadcasted_iota(jnp.int32, (48, 128), 1) < 64
    hidden_ref[...] = jnp.where(left, turned[:48], turned[48:96])


def select(where, parts):
    return pl.pallas_call(
        select_kernel,
        in_specs=[smem_spec()] + [vmem_spec()] * 4,
        out_specs=[vmem_spec()] * 2,
        out_shape=[shape((192, 128)), shape((48, 128), F32)],
        scratch_shapes=[pltpu.VMEM((4,) + parts[0].shape, BF16)],
        cost_estimate=cost(2 * 192 * 1088 * 128, MIB),
        compiler_params=params(),
        name="select",
    )(where, *parts)


def split_out_kernel(where_ref, mine_ref, theirs_ref, after_ref, *out_refs):
    core = where_ref[0]
    row = lax.broadcasted_iota(jnp.int32, (192, 384), 0)
    lane = lax.broadcasted_iota(jnp.int32, (192, 384), 1)
    pick = one_hot(lane == row // 96 * 192 + row % 96 + core * 96)
    for part in range(8):
        for weight_ref, out_ref in zip((mine_ref, theirs_ref), out_refs):
            weight = weight_ref[:, part * 384 : part * 384 + 384]
            out_ref[2 * part : 2 * part + 2] = nt_dot(pick, weight).astype(BF16).reshape(2, 96, 128)


def split_out(where, mine, theirs, after):
    return pl.pallas_call(
        split_out_kernel,
        grid=(2,),
        in_specs=[smem_spec()] + [pl.BlockSpec((128, 3072), lambda i: (0, i))] * 2 + [any_spec()],
        out_specs=[pl.BlockSpec((16, 96, 128), lambda i: (i, 0, 0))] * 2,
        out_shape=[shape((NX * NZ, 96, 128))] * 2,
        cost_estimate=cost(2 * 16 * 384 * 384 * 128, 3 * MIB),
        compiler_params=params(),
        name="split_out",
    )(where, mine, in_hbm(theirs), after)


def own_blocks(core):
    row = lax.broadcasted_iota(jnp.int32, (768, 384), 0)
    lane = lax.broadcasted_iota(jnp.int32, (768, 384), 1)
    return one_hot(row == lane // 96 * 192 + lane % 96 + core * 96)


def split_down_kernel(where_ref, mine_ref, theirs_ref, after_ref, *out_refs):
    pick = own_blocks(where_ref[0])
    for part in range(2):
        for weight_ref, out_ref in zip((mine_ref, theirs_ref), out_refs):
            weight = weight_ref[:, part * 768 : part * 768 + 768]
            out_ref[:, part * 384 : part * 384 + 384] = jnp.dot(weight, pick, preferred_element_type=F32).astype(BF16)


def split_down(where, mine, theirs, after):
    hidden = mine.shape[0]
    weights = pl.BlockSpec((hidden, 1536), lambda i, where: (0, lax.rem(where[1] + i, NX)))
    return pl.pallas_call(
        split_down_kernel,
        grid_spec=pltpu.PrefetchScalarGridSpec(
            num_scalar_prefetch=1,
            grid=(NX,),
            in_specs=[weights, weights, any_spec()],
            out_specs=[pl.BlockSpec((hidden, NZ * 96), lambda i, where: (0, i))] * 2,
        ),
        out_shape=[shape((hidden, NX * NZ * 96))] * 2,
        cost_estimate=cost(2 * 16 * 384 * 512 * 144, 4 * MIB),
        compiler_params=params(),
        name="split_down",
    )(where, mine, in_hbm(theirs), after)


def split_up_kernel(where_ref, mine_ref, theirs_ref, after_ref, out_ref, done_ref):
    done_ref[...] = jnp.zeros_like(done_ref)
    pick = own_blocks(where_ref[0])
    rows = mine_ref.shape[0]
    for part in range(2):
        for side, weight_ref in enumerate((mine_ref, theirs_ref)):
            weight = weight_ref[:, part * 768 : part * 768 + 768]
            out_ref[side * rows : (side + 1) * rows, part * 384 : part * 384 + 384] = jnp.dot(
                weight, pick, preferred_element_type=F32
            ).astype(BF16)


def split_up(where, mine, theirs, after):
    rows, width = mine.shape
    weights = pl.BlockSpec((rows, 1536), lambda i: (0, i))
    return pl.pallas_call(
        split_up_kernel,
        grid=(width // 1536,),
        in_specs=[smem_spec(), weights, weights, any_spec()],
        out_specs=[pl.BlockSpec((2 * rows, 768), lambda i: (0, i)), pl.BlockSpec((8, 128), lambda i: (0, 0))],
        out_shape=[shape((2 * rows, width // 2)), shape((8, 128), F32)],
        cost_estimate=cost(2 * 576 * 6144 * 768, 11 * MIB),
        compiler_params=params(16),
        name="split_up",
    )(where, in_hbm(mine), in_hbm(theirs), after)


def project_kernel(keep_ref, other_ref, mine_ref, theirs_ref, out_ref):
    blocks = keep_ref.shape[0]
    mine, theirs = mine_ref[:64], theirs_ref[:64]
    total = nt_dot(keep_ref[...].reshape(blocks * 96, 128), jnp.concatenate([mine, mine], 0))
    total += nt_dot(other_ref[...].reshape(blocks * 96, 128), jnp.concatenate([theirs, theirs], 0))
    total = total.reshape(blocks, 96, 128)
    left = lax.broadcasted_iota(jnp.int32, (blocks, 48, 128), 2) < 64
    total = jnp.where(left, total[:, :48], total[:, 48:]).astype(BF16)
    for column in range(blocks // NZ):
        out_ref[:, column] = total[column * NZ : (column + 1) * NZ]


def project(keep, other, mine, theirs):
    block = 16
    weights = pl.BlockSpec((block, 96, 128), lambda i: (i, 0, 0))
    tokens = pl.BlockSpec((192, 128), lambda i: (0, 0))
    return pl.pallas_call(
        project_kernel,
        grid=(NX * NZ // block,),
        in_specs=[weights, weights, tokens, tokens],
        out_specs=pl.BlockSpec((NZ, block // NZ, 48, 128), lambda i: (0, i, 0, 0)),
        out_shape=shape((NZ, NX, 48, 128)),
        cost_estimate=cost(2 * 3072 * 256 * 128, 2 * MIB),
        compiler_params=params(),
        name="project",
    )(keep, other, mine, theirs)


def project_rest_kernel(where_ref, keep_ref, other_ref, mine_ref, theirs_ref, after_ref, *out_refs):
    for far, out_ref in enumerate(out_refs):
        start = lax.rem(where_ref[1] + far, NX) * NZ
        total = nt_dot(keep_ref[pl.ds(start, NZ)].reshape(NZ * 96, 128), mine_ref[64:])
        total += nt_dot(other_ref[pl.ds(start, NZ)].reshape(NZ * 96, 128), theirs_ref[64:])
        out_ref[...] = total.astype(BF16).reshape(NZ, 96, 128)


def project_rest(where, keep, other, mine, theirs, after):
    return pl.pallas_call(
        project_rest_kernel,
        in_specs=[smem_spec()] + [vmem_spec()] * 4 + [any_spec()],
        out_specs=[vmem_spec()] * NX,
        out_shape=[shape((NZ, 96, 128))] * NX,
        cost_estimate=cost(2 * 3072 * 256 * 128, 3 * MIB),
        compiler_params=params(),
        name="project_rest",
    )(where, keep, other, mine, theirs, after)


def add_rest_kernel(*refs):
    in_refs, out_ref = refs[:-1], refs[-1]
    blank = jnp.zeros((32, 128), F32)
    for block in range(NZ):
        total = sum(in_ref[block].astype(F32) for in_ref in in_refs)
        total = jnp.concatenate([total, blank], 0).T
        out_ref[:, block] = total.astype(BF16).reshape(4, 32, 128)


def add_rest(parts):
    return pl.pallas_call(
        add_rest_kernel,
        in_specs=[vmem_spec()] * NX,
        out_specs=vmem_spec(),
        out_shape=shape((4, NZ, 32, 128)),
        cost_estimate=cost(MIB, MIB),
        compiler_params=params(),
        name="add_rest",
    )(*parts)


def residual_kernel(in_ref, hidden_ref, one_ref, two_ref, three_ref, send_ref):
    routed = (jnp.sum(in_ref[...].astype(F32), 0) + hidden_ref[...]).astype(BF16)
    for copy in range(send_ref.shape[0]):
        send_ref[copy] = routed


def routed_residual(parts, hidden, *after):
    return pl.pallas_call(
        residual_kernel,
        in_specs=[vmem_spec()] * 2 + [any_spec()] * 3,
        out_specs=vmem_spec(),
        out_shape=shape((NX * NZ, 48, 128)),
        cost_estimate=cost(MIB, MIB),
        compiler_params=params(),
        name="routed_residual",
    )(parts, hidden, *after)


def up_kernel(features_ref, weight_ref, after_ref, out_ref):
    rows, blocks = weight_ref.shape[0], features_ref.shape[0]
    step = blocks // 2
    left = lax.broadcasted_iota(jnp.int32, (48, 128), 1) < 64
    zero = jnp.zeros((48, 128), BF16)
    total = jnp.zeros((rows, 128), F32)
    square = jnp.zeros((8, 128), F32)
    for start in range(0, blocks, step):
        pieces = []
        for block in range(start, start + step):
            part = features_ref[block % NZ * NX + block // NZ]
            pieces += [jnp.where(left, part, zero), jnp.where(left, zero, part)]
            wide = part.astype(F32)
            square += jnp.sum((wide * wide).reshape(6, 8, 128), 0)
        weight = weight_ref[:, start * 96 : (start + step) * 96]
        total += jnp.dot(weight, jnp.concatenate(pieces, 0), preferred_element_type=F32)
    square = jnp.broadcast_to(jnp.sum(square, 0, keepdims=True), (8, 128))
    out_ref[:rows] = total[:, :64] + total[:, 64:]
    out_ref[rows:] = square[:, :64] + square[:, 64:]


def up_project(features, weight, after):
    rows = weight.shape[0]
    return pl.pallas_call(
        up_kernel,
        in_specs=[vmem_spec(), vmem_spec(), any_spec()],
        out_specs=vmem_spec(),
        out_shape=shape((rows + 8, 64), F32),
        cost_estimate=cost(2 * 576 * 3072 * 128, 5 * MIB),
        compiler_params=params(16),
        name="up_project",
    )(features, weight, after)


def down_kernel(mine_ref, theirs_ref, keep_ref, other_ref, *out_refs):
    rows = (mine_ref.shape[0] - 8) // 2
    square = mine_ref[2 * rows : 2 * rows + 1] + theirs_ref[2 * rows : 2 * rows + 1]
    scale = lax.rsqrt(square / 6144.0 + EPSILON_NORM)
    total = jnp.zeros((64, keep_ref.shape[1]), F32)
    for one, two, weight_ref in ((0, rows, keep_ref), (rows, 0, other_ref)):
        product = (mine_ref[one : one + rows] + theirs_ref[two : two + rows]) * scale
        hidden = (silu(product[: rows // 2]) * product[rows // 2 :]).astype(BF16)
        total += tn_dot(hidden, weight_ref[...])
    total = total.astype(BF16)
    width = NZ * 96
    for step in range(2):

        @pl.when(pl.program_id(0) == step)
        def _():
            for column in range(2):
                out_refs[2 * step + column][...] = total[:, column * width : (column + 1) * width]


def down_project(mine, theirs, keep, other):
    hidden, width = keep.shape
    products = pl.BlockSpec(mine.shape, lambda i: (0, 0))
    weights = pl.BlockSpec((hidden, width // 2), lambda i: (0, i))
    return pl.pallas_call(
        down_kernel,
        grid=(2,),
        in_specs=[products, products, weights, weights],
        out_specs=[pl.BlockSpec((64, NZ * 96), lambda i: (0, 0))] * NX,
        out_shape=[shape((64, NZ * 96))] * NX,
        cost_estimate=cost(2 * 288 * 3072 * 64, 3 * MIB),
        compiler_params=params(16),
        name="down_project",
    )(mine, theirs, keep, other)


def merge_kernel(rest_ref, *refs):
    in_refs, out_ref = refs[:-1], refs[-1]
    for block in range(NZ):
        out_ref[block, :, :32] = rest_ref[:, block]
    row = lax.broadcasted_iota(jnp.int32, (384, 512), 0)
    lane = lax.broadcasted_iota(jnp.int32, (384, 512), 1)
    spread = one_hot((row == lane // 128 * 96 + lane % 128) & (lane % 128 < 96))
    for half in range(2):
        total = sum(in_ref[:, half * 384 : half * 384 + 384].astype(F32) for in_ref in in_refs).astype(BF16)
        total = jnp.dot(total, spread, preferred_element_type=F32).astype(BF16)
        for block in range(4):
            part = total[:, block * 128 : block * 128 + 128]
            out_ref[half * 4 + block, :, 32:] = part.reshape(4, 16, 128)


def merge(rest, parts):
    return pl.pallas_call(
        merge_kernel,
        in_specs=[vmem_spec()] * (1 + NX),
        out_specs=vmem_spec(),
        out_shape=shape((NZ, 4, 48, 128)),
        cost_estimate=cost(MIB, MIB),
        compiler_params=params(),
        name="merge",
    )(rest, *parts)


def combine_kernel(parts_ref, place_ref, weight_ref, hidden_ref, out_ref):
    parts = jnp.sum(parts_ref[...].astype(F32), 0)
    residual = hidden_ref[...].astype(F32) + parts[:, :32].reshape(128, 128)
    result = parts[:, 32:].astype(BF16).reshape(64, 128)
    fetched = jnp.dot(place_ref[:, :64], result, preferred_element_type=F32)
    out_ref[...] = (residual + weight_ref[...] * fetched)[:, :96].astype(BF16)


def combine(parts, place, weight, hidden):
    return pl.pallas_call(
        combine_kernel,
        in_specs=[vmem_spec()] * 4,
        out_specs=vmem_spec(),
        out_shape=shape((128, 96)),
        cost_estimate=cost(MIB, MIB),
        compiler_params=params(),
        name="combine",
    )(parts, place, weight, hidden)


def gate_kernel(value_ref, after_ref, out_ref):
    out_ref[...] = value_ref[...]


def gate(value, after):
    return pl.pallas_call(
        gate_kernel,
        in_specs=[vmem_spec(), any_spec()],
        out_specs=vmem_spec(),
        out_shape=jax.ShapeDtypeStruct(value.shape, value.dtype),
        compiler_params=params(4),
        name="gate",
    )(value, after)


def swap(value):
    return lax.ppermute(value, "core", [(0, 1), (1, 0)])


def shifted(blocks, axis):
    count = len(blocks)
    return [blocks[0]] + [
        lax.ppermute(blocks[far], axis, [(i, (i + far) % count) for i in range(count)]) for far in range(1, count)
    ]


def per_device(
    unfinished, states, qkv_rows, decay_rate, out_weight, hidden_in, routes, route_weight, expert_up, expert_down
):
    where = jnp.stack([lax.axis_index(axis).astype(jnp.int32) for axis in ("core", "x", "dp")])

    with jax.named_scope("attention"):
        local = attend(states[0], qkv_rows[0].transpose(0, 2, 1, 3))
        parts = lax.all_to_all(local, HEAD, 0, 0, tiled=True)
    with jax.named_scope("weights"):
        keep_out, other_out = split_out(where, out_weight, swap(out_weight), local)
    with jax.named_scope("routing"):
        hidden = jnp.pad(hidden_in.transpose(1, 2, 0).reshape(128, 96), ((0, 0), (0, 32)))
        slots = jnp.repeat(unfinished, 4)[:, None]
        place, weight, facts = route(routes.reshape(128, 2), route_weight.reshape(128, 2), hidden, slots)
    with jax.named_scope("heads"):
        head_out = decay_heads(where, decay_rate, parts, facts, keep_out)
        head_rows = [rows.reshape(-1, 128) for rows in shifted(head_out, "dp")]
        mine, routed_hidden = select(where, head_rows)
        theirs = swap(mine)
    with jax.named_scope("projection"):
        partial = project(keep_out, other_out, mine, theirs)
        summed = lax.all_to_all(partial.reshape(NZ * NX, 48, 128), ("z", "x"), 0, 0, tiled=True)
        keep_down, other_down = split_down(where, expert_down[0], swap(expert_down[0]), partial)
        rest = project_rest(where, keep_out, other_out, mine, theirs, partial)
        rest = shifted(rest, "x")
        routed = routed_residual(summed, routed_hidden, rest[1], rest[3], keep_down)
    with jax.named_scope("expert"):
        up = expert_up[0].transpose(1, 2, 0).reshape(288, 6144)
        up, split = split_up(where, up, swap(up), routed)
        features = gate(lax.all_to_all(routed, ("z", "x"), 0, 0, tiled=True), rest[2])
        products = up_project(features, up, swap(split))
        results = down_project(products, swap(products), keep_down, other_down)
        rest = add_rest(rest)
        merged = merge(rest, shifted(results, "x")).reshape(32, 48, 128)
        returned = lax.all_to_all(merged, ("z", "dp"), 0, 0, tiled=True)
    with jax.named_scope("output"):
        mixed = combine(returned.reshape(NZ, 4, 48, 128), place, weight, hidden)
        return mixed.reshape(32, 4, 96).transpose(2, 0, 1)


def solution(mesh):
    grid = Mesh(mesh.devices.reshape(mesh.shape["dp"], NX, NZ, NC), EVERY)
    return jax.shard_map(
        per_device,
        mesh=grid,
        in_specs=(
            P("dp"),
            P(EVERY, None, None, None),
            P(EVERY, None, None, None, None),
            P(HEAD),
            P(HEAD, None),
            P(HEAD, "dp", None),
            P("dp", None, None),
            P("dp", None, None),
            P("dp", None, None, HEAD),
            P("dp", HEAD, None),
        ),
        out_specs=P(HEAD, "dp", None),
        check_vma=False,
    )
```
